32 devices in a mesh: dp: 8 (over z, core), tensor: 4 (over y, x).
Axes of the slice: x: 2, y: 2, z: 4, core: 2. Of those that a mesh axis runs over, the one named last changes fastest.
Arguments:
- tokens: bfloat16 [8, 1024, 2048], P('dp', 'tensor'), may hold values from -6 to 6
- cotangent: bfloat16 [8, 1024, 2048], P('dp', 'tensor'), may hold values from -6 to 6
- w_query: bfloat16 [2048, 2048], P(None, 'tensor'), may hold values from -0.1875 to 0.1875
- w_key: bfloat16 [2048, 1024], P(None, 'tensor'), may hold values from -0.1875 to 0.1875
- w_value: bfloat16 [2048, 1024], P(None, 'tensor'), may hold values from -0.125 to 0.125
- w_output: bfloat16 [2048, 2048], P('tensor'), may hold values from -0.375 to 0.375
- w_gate: bfloat16 [2048, 5632], P(None, 'tensor'), may hold values from -0.125 to 0.125
- w_up: bfloat16 [2048, 5632], P(None, 'tensor'), may hold values from -0.125 to 0.125
- w_down: bfloat16 [5632, 2048], P('tensor'), may hold values from -0.078125 to 0.078125
- gain_attn: float32 [2048], replicated, may hold values from 0.5 to 1.5
- gain_mlp: float32 [2048], replicated, may hold values from 0.5 to 1.5
- dropped: int32 [8], P('dp'), may hold values 0 or 1
- exit_scale: float32 [8], P('dp'), may hold values from 0.5 to 2
- positions: int32 [8, 1024], P('dp'), may hold values from 0 to 1023, as said below
Outputs:
- mixed: bfloat16 [8, 1024, 2048], P('dp', 'tensor')
- input_grad: float32 [8, 1024, 2048], P('dp', 'tensor')
- grad_query: float32 [2048, 2048], P(None, 'tensor')
- grad_key: float32 [2048, 1024], P(None, 'tensor')
- grad_value: float32 [2048, 1024], P(None, 'tensor')
- grad_output: float32 [2048, 2048], P('tensor')
- grad_gate: float32 [2048, 5632], P(None, 'tensor')
- grad_up: float32 [2048, 5632], P(None, 'tensor')
- grad_down: float32 [5632, 2048], P('tensor')
- grad_gain_attn: float32 [2048], replicated
- grad_gain_mlp: float32 [2048], replicated
The draws below stay inside these ranges and needn't reach their ends.
Inputs may be any that keep to these rules, and one draw needn't show every extreme that they name: Each sequence is cut into up to four documents, and positions count from 0 at each document's start; one sequence, drawn from the seed, is a single document.
All inputs are finite; a program needn't handle non-finite values. No bound on the sum of `dropped` on one device may be relied on, other than what follows from the above.
Results may differ from the reference program's by a relative error of at most 0.015.
Values may be sent and summed in bfloat16 or wider, within the bound.
No kernel may reach another device: no remote copies, remote signals or barrier semaphores. Data moves between devices by JAX's collectives and lax.ppermute only.
A program may use at most 320 MiB of HBM per device.

```python
import math
import jax
import jax.numpy as jnp
from jax import lax

D = 2048
H = 16
KV = 8
HD = 128
FF = 5632
SEQ = 1024
SEQS = 8


def draw_positions(key, part):
    key = jax.random.fold_in(key, 11)
    cut_points = jax.random.randint(jax.random.fold_in(key, 1), (SEQS, 3), 1, SEQ)
    single_doc = jax.random.randint(jax.random.fold_in(key, 2), (), 0, SEQS)
    seq_ids = jnp.arange(SEQS, dtype=jnp.int32)[:, None]
    cut_points = jnp.where(seq_ids == single_doc, 0, cut_points)
    token_ids = jnp.arange(SEQ, dtype=jnp.int32)
    begins = jnp.max(jnp.where(cut_points[:, :, None] <= token_ids[None, None, :], cut_points[:, :, None], 0), axis=1)
    return (token_ids[None, :] - begins).astype(jnp.int32)


def plant(array, key, smallest, top_value):
    dims = array.shape
    place = [jax.random.randint(jax.random.fold_in(key, axis), (), 0, dims[axis]) for axis in range(len(dims))]
    array = array.at[tuple(place)].set(smallest)
    longest = dims.index(max(dims))
    place[longest] = (place[longest] + 1) % dims[longest]
    return array.at[tuple(place)].set(top_value)


def level_of(own_key, dims, split, low, largest):
    loudness = 1.0
    for dim, shards_of in split:
        steps = jax.random.uniform(jax.random.fold_in(jax.random.fold_in(own_key, 6), dim), (shards_of,), jnp.float32, low / len(split), largest / len(split))
        loudness = loudness * jnp.repeat(jnp.exp(steps), dims[dim] // shards_of).reshape((-1,) + (1,) * (len(dims) - 1 - dim))
    return loudness


def gaussian(key, dims, width, bound, shards=(), held_as=jnp.bfloat16):
    loudness = level_of(key, dims, shards, -0.22, 0.18) if shards else 1.0
    array = jax.random.normal(key, dims, jnp.float32) * width * loudness
    return jnp.minimum(jnp.maximum(array, -bound), bound).astype(held_as)


def setup_inputs(seed: int = 0) -> dict:
    splits = jax.random.split(jax.random.key(seed), 15)
    tokens = gaussian(splits[0], (SEQS, SEQ, D), 1.0, 6.0, ((0, 8), (1, 4)))
    cotangent = gaussian(splits[1], (SEQS, SEQ, D), 1.0, 6.0, ((0, 8), (1, 4)))
    w_query = gaussian(splits[2], (D, H * HD), (D // 2) ** -0.5, 0.1875, ((1, 4),))
    w_key = gaussian(splits[3], (D, KV * HD), (D // 2) ** -0.5, 0.1875, ((1, 4),))
    w_value = gaussian(splits[4], (D, KV * HD), D ** -0.5, 0.125, ((1, 4),))
    w_output = gaussian(splits[5], (H * HD, D), (2 * HD) ** -0.5, 0.375, ((0, 4),))
    w_gate = gaussian(splits[6], (D, FF), D ** -0.5, 0.125, ((1, 4),))
    w_up = gaussian(splits[7], (D, FF), D ** -0.5, 0.125, ((1, 4),))
    w_down = gaussian(splits[8], (FF, D), FF ** -0.5, 0.078125, ((0, 4),))
    gain_attn = jnp.clip(1.0 + 0.1 * jax.random.normal(splits[9], (D,), jnp.float32), 0.5, 1.5)
    gain_mlp = jnp.clip(1.0 + 0.1 * jax.random.normal(splits[10], (D,), jnp.float32), 0.5, 1.5)
    dropped = plant((jax.random.randint(splits[11], (SEQS,), 0, 4) < 1).astype(jnp.int32), jax.random.fold_in(splits[11], 1), 0, 1)
    exit_scale = jnp.clip(jnp.exp(math.log(2.0) - 1.3862944 * jax.random.uniform(splits[12], (SEQS,), jnp.float32) ** level_of(splits[12], (SEQS,), ((0, 8),), -0.2, 0.2)), 0.5, 2.0)
    positions = draw_positions(jax.random.fold_in(splits[14], 71), 0)
    return {"tokens": tokens, "cotangent": cotangent, "w_query": w_query, "w_key": w_key, "w_value": w_value, "w_output": w_output, "w_gate": w_gate, "w_up": w_up, "w_down": w_down, "gain_attn": gain_attn, "gain_mlp": gain_mlp, "dropped": dropped, "exit_scale": exit_scale, "positions": positions}


@jax.custom_vjp
def low(v):
    return lax.optimization_barrier(v.astype(jnp.bfloat16)).astype(jnp.float32)

@jax.custom_vjp
def low_back(v):
    return v

def low_keep(v):
    return (low(v), None)

def low_pass(kept, grad):
    return (grad,)

def back_keep(v):
    return (v, None)

def back_low(kept, grad):
    return (low(grad),)
low.defvjp(low_keep, low_pass)
low_back.defvjp(back_keep, back_low)

def rms_scale(hidden_in, gain_vec):
    return hidden_in * lax.rsqrt(lax.optimization_barrier(jnp.mean(hidden_in * hidden_in, axis=-1, keepdims=True)) + 1e-05) * gain_vec

def angle_tables(pos_ids, head_width):
    freqs = jnp.exp(jnp.arange(head_width // 2, dtype=jnp.float32) * (-2.0 * math.log(10000.0) / head_width))
    turned = pos_ids.astype(jnp.float32)[:, None] * freqs[None, :]
    return (jnp.cos(turned), jnp.sin(turned))

def rotate(vectors, cos_table, sin_table):
    half_width = vectors.shape[-1] // 2
    first = vectors[..., :half_width]
    second = vectors[..., half_width:]
    cos_part = cos_table[:, None, :]
    sin_part = sin_table[:, None, :]
    return jnp.concatenate([first * cos_part - second * sin_part, second * cos_part + first * sin_part], axis=-1)

def layer(inputs, wq_full, wk_full, wv_full, wo_full, wg_full, wu_full, wd_full, gain_one, gain_two, survive, cos_table, sin_table):
    highest = lax.Precision.HIGHEST
    share = H // KV
    n_one = low(rms_scale(inputs, gain_one))
    query_heads = low(rotate(low_back(jnp.dot(n_one, wq_full, precision=highest)).reshape(SEQ, H, HD), cos_table, sin_table))
    key_heads = low(rotate(low_back(jnp.dot(n_one, wk_full, precision=highest)).reshape(SEQ, KV, HD), cos_table, sin_table))
    value_heads = low(low_back(jnp.dot(n_one, wv_full, precision=highest))).reshape(SEQ, KV, HD)
    grouped = query_heads.reshape(SEQ, KV, share, HD)
    block_rows = min(512, SEQ)
    factor = 1.0 / math.sqrt(HD)

    def attend(first_row):
        query_block = lax.dynamic_slice_in_dim(grouped, first_row, block_rows, 0)
        raw_scores = low_back(jnp.einsum('qkgd,skd->kgqs', query_block, key_heads, precision=highest) * factor)
        row_ids = first_row + jnp.arange(block_rows, dtype=jnp.int32)[:, None]
        col_ids = jnp.arange(SEQ, dtype=jnp.int32)[None, :]
        masked = jnp.where(col_ids <= row_ids, raw_scores, -1e+30)
        powers = jnp.exp(masked - lax.optimization_barrier(jnp.max(masked, axis=-1, keepdims=True)))
        prob_rows = powers / lax.optimization_barrier(jnp.sum(powers, axis=-1, keepdims=True))
        return jnp.einsum('kgqs,skd->qkgd', low(prob_rows), value_heads, precision=highest)
    starts = jnp.arange(SEQ // block_rows, dtype=jnp.int32) * block_rows
    attended = lax.map(jax.checkpoint(attend), starts).reshape(SEQ, H * HD)
    attn_bf = low(low_back(attended))
    h_one = inputs + survive * low_back(jnp.dot(attn_bf, wo_full, precision=highest))
    n_two = low(rms_scale(h_one, gain_two))
    gate_proj = low_back(jnp.dot(n_two, wg_full, precision=highest))
    up_proj = low_back(jnp.dot(n_two, wu_full, precision=highest))
    hidden = low(gate_proj * jax.nn.sigmoid(gate_proj) * up_proj)
    return h_one + survive * low_back(jnp.dot(hidden, wd_full, precision=highest))

def reference(tokens, cotangent, w_query, w_key, w_value, w_output, w_gate, w_up, w_down, gain_attn, gain_mlp, dropped, exit_scale, positions):
    params = tuple((weight_arr.astype(jnp.float32) for weight_arr in (w_query, w_key, w_value, w_output, w_gate, w_up, w_down, gain_attn, gain_mlp)))

    def one_sequence(running, per_seq):
        seq_tokens, seq_cot, drop_flag, exit_factor, pos_ids = per_seq
        survive = 1.0 - drop_flag.astype(jnp.float32)
        cos_table, sin_table = angle_tables(pos_ids, HD)

        def forward(inputs, *weights_in):
            return layer(inputs, *weights_in, survive, cos_table, sin_table)
        result, pull_back = jax.vjp(forward, seq_tokens.astype(jnp.float32), *params)
        gradients = pull_back(seq_cot.astype(jnp.float32) * exit_factor)
        updated = tuple((total + piece for total, piece in zip(running, gradients[1:])))
        return (updated, (result.astype(jnp.bfloat16), gradients[0]))
    zero_grads = tuple((jnp.zeros_like(weight_arr) for weight_arr in params))
    totals, outputs = lax.scan(one_sequence, zero_grads, (tokens, cotangent, dropped, exit_scale, positions))
    return (outputs[0], outputs[1], totals[0], totals[1], totals[2], totals[3], totals[4], totals[5], totals[6], totals[7], totals[8])
```

```python
import math

import jax
import jax.numpy as jnp
from jax import lax
from jax.sharding import PartitionSpec as P

HD = 128
F32 = jnp.float32
BF16 = jnp.bfloat16


def dot(a, b, dims):
    return lax.dot_general(a, b, (dims, ((), ())), preferred_element_type=F32)


def dot_nn(a, b):
    return dot(a, b, ((1,), (0,)))


def dot_nt(a, b):
    return dot(a, b, ((1,), (1,)))


def dot_tn(a, b):
    return dot(a, b, ((0,), (0,)))


def rms_scale(hidden_in, gain_vec):
    return (
        hidden_in
        * lax.rsqrt(jnp.mean(hidden_in * hidden_in, axis=-1, keepdims=True) + 1e-05)
        * gain_vec
    )


def gain_part(hidden_in, grad_rows):
    normed = hidden_in * lax.rsqrt(jnp.mean(hidden_in * hidden_in, axis=-1, keepdims=True) + 1e-05)
    return jnp.sum(grad_rows * normed, axis=0)


def angle_tables(pos_ids, head_width):
    freqs = jnp.exp(
        jnp.arange(head_width // 2, dtype=F32) * (-2.0 * math.log(10000.0) / head_width)
    )
    turned = pos_ids.astype(F32)[:, None] * freqs[None, :]
    return (jnp.cos(turned), jnp.sin(turned))


def rotate(vectors, cos_table, sin_table):
    half_width = vectors.shape[-1] // 2
    first = vectors[..., :half_width]
    second = vectors[..., half_width:]
    cos_part = cos_table[:, None, :]
    sin_part = sin_table[:, None, :]
    return jnp.concatenate(
        [first * cos_part - second * sin_part, second * cos_part + first * sin_part], axis=-1
    )


def swap(value, axis, size, bit):
    return lax.ppermute(value, axis, [(i, i ^ bit) for i in range(size)])


class Rows:
    def __init__(self, size):
        self.size = size
        self.square = size == 4
        me = lax.axis_index("tensor")
        self.ids = [me ^ r for r in range(4)] if self.square else list(range(size))

    def swap(self, value, bit):
        return swap(value, "tensor", self.size, bit)

    def gather(self, block):
        if not self.square:
            whole = lax.all_gather(block, "tensor", axis=0, tiled=True)
            return jnp.split(whole, self.size, axis=0)
        half = block.shape[0] // 2
        top, low = block[:half], block[half:]
        x_top, y_low = self.swap(top, 1), self.swap(low, 2)
        x_low, y_top = self.swap(low, 1), self.swap(top, 2)
        d_top, d_low = self.swap(x_top, 2), self.swap(y_low, 1)
        return [
            block,
            jnp.concatenate([x_top, x_low]),
            jnp.concatenate([y_top, y_low]),
            jnp.concatenate([d_top, d_low]),
        ]

    def scatter(self, parts):
        if not self.square:
            whole = jnp.concatenate(parts, axis=0)
            return lax.psum_scatter(whole, "tensor", scatter_dimension=0, tiled=True).astype(F32)
        own, x_part, y_part, d_part = parts
        half = own.shape[0] // 2
        y_top = self.swap(d_part[:half], 1)
        x_low = self.swap(d_part[half:], 2)
        x_got_top = self.swap(x_part[:half], 1)
        y_got_low = self.swap(y_part[half:], 2)
        x_got_low = self.swap(add(x_part[half:], x_low), 1)
        y_got_top = self.swap(add(y_part[:half], y_top), 2)
        x_got = jnp.concatenate([x_got_top, x_got_low]).astype(F32)
        y_got = jnp.concatenate([y_got_top, y_got_low]).astype(F32)
        return own.astype(F32) + x_got + y_got


def add(a, b):
    return (a.astype(F32) + b.astype(F32)).astype(BF16)


class Sums:
    def __init__(self, size):
        self.size = size
        self.line = size == 8
        where = lax.axis_index("dp")
        self.core = where % 2
        z = where // 2
        self.middle = (z == 1) | (z == 2)

    def hop(self, value, steps):
        pairs = [(2 * a + c, 2 * b + c) for a, b in steps for c in range(2)]
        return lax.ppermute(value, "dp", pairs)

    def halves(self, left, right, axis, start, count):
        half = count // 2
        outs = []
        for pick in (1 - self.core, self.core):
            at = start + pick * half
            if axis == 0:
                outs.append((lax.dynamic_slice_in_dim(left, at, half, 1), right))
            else:
                outs.append((left, lax.dynamic_slice_in_dim(right, at, half, 1)))
        other = dot_tn(*outs[0]).astype(BF16)
        got = swap(other, "dp", self.size, 1)
        return (dot_tn(*outs[1]) + got.astype(F32)).astype(BF16)

    def run(self, jobs):
        if not self.line:
            return [
                lax.psum(dot_tn(left, right).astype(BF16), "dp").astype(F32)
                for left, right, _, _ in jobs
            ]
        todo = []
        for job, (left, right, axis, chunks) in enumerate(jobs):
            total = (left, right)[axis].shape[1]
            step = total // chunks
            for k in range(chunks):
                todo.append((job, axis, k * step, step))
        held, fold, mids, ends, done = {}, {}, {}, {}, {}
        count = len(todo)
        token = None

        def after(*values):
            if token is None:
                return values
            return lax.optimization_barrier((token, *values))[1:]

        for s in range(-1, count + 3):
            if s + 1 < count:
                job, axis, start, step = todo[s + 1]
                left, right = jobs[job][:2]
                held[s + 1] = self.halves(left, right, axis, start, step)
                fold[s + 1] = self.hop(held[s + 1], [(0, 1), (3, 2)])
            if 0 <= s < count:
                mine, got = after(held[s], fold[s])
                held[s] = token = add(mine, got)
                mids[s] = self.hop(held[s], [(1, 2), (2, 1)])
            if 0 <= s - 1 < count:
                mine, got = after(held[s - 1], mids[s - 1])
                held[s - 1] = token = add(mine, got)
                ends[s - 1] = self.hop(held[s - 1], [(1, 0), (2, 3)])
            if 0 <= s - 2 < count:
                mine, got = after(held[s - 2], ends[s - 2])
                held[s - 2] = token = jnp.where(self.middle, mine, got)
                done[s - 2] = swap(held[s - 2], "dp", self.size, 1)
        outs = []
        for job, (left, right, axis, chunks) in enumerate(jobs):
            pieces = []
            for s, what in enumerate(todo):
                if what[0] == job:
                    first = jnp.where(self.core == 0, held[s], done[s])
                    second = jnp.where(self.core == 0, done[s], held[s])
                    pieces += [first, second]
            outs.append(jnp.concatenate(pieces, axis=axis).astype(F32))
        return outs


def psum_small(value, mesh_shape):
    for axis in ("dp", "tensor"):
        size = mesh_shape[axis]
        if size & (size - 1):
            value = lax.psum(value, axis)
            continue
        bit = 1
        while bit < size:
            value = value + swap(value, axis, size, bit)
            bit *= 2
    return value


def local(
    mesh_shape,
    tokens,
    cotangent,
    w_query,
    w_key,
    w_value,
    w_output,
    w_gate,
    w_up,
    w_down,
    gain_attn,
    gain_mlp,
    dropped,
    exit_scale,
    positions,
):
    rows = Rows(mesh_shape["tensor"])
    sums = Sums(mesh_shape["dp"])
    ids = rows.ids
    survive = 1.0 - dropped[0].astype(F32)
    x_rows = tokens[0].astype(F32)
    cot_rows = cotangent[0].astype(F32) * exit_scale[0]
    own_rows = x_rows.shape[0]
    seq_len = own_rows * len(ids)
    n_one_own = rms_scale(x_rows, gain_attn).astype(BF16)
    n_one_parts = rows.gather(n_one_own)
    grad_m_parts = rows.gather((survive * cot_rows).astype(BF16))
    pos_parts = [lax.dynamic_slice_in_dim(positions[0], i * own_rows, own_rows) for i in ids]
    place = jnp.concatenate([i * own_rows + jnp.arange(own_rows, dtype=jnp.int32) for i in ids])
    cos_table, sin_table = angle_tables(jnp.concatenate(pos_parts), HD)
    local_heads = w_query.shape[1] // HD
    local_kv = w_key.shape[1] // HD
    share = local_heads // local_kv
    factor = 1.0 / math.sqrt(HD)

    def part(table, j):
        return table[j * own_rows : (j + 1) * own_rows]

    q_parts, k_parts, v_parts = [], [], []
    for j, block in enumerate(n_one_parts):
        cos_part, sin_part = part(cos_table, j), part(sin_table, j)
        q_parts.append(
            rotate(dot_nn(block, w_query).reshape(own_rows, local_heads, HD), cos_part, sin_part)
            .astype(BF16)
            .reshape(own_rows, local_kv, share, HD)
        )
        k_parts.append(
            rotate(
                dot_nn(block, w_key).reshape(own_rows, local_kv, HD), cos_part, sin_part
            ).astype(BF16)
        )
        v_parts.append(dot_nn(block, w_value).astype(BF16).reshape(own_rows, local_kv, HD))
    key_heads = jnp.concatenate(k_parts)
    value_heads = jnp.concatenate(v_parts)

    def block_scores(query_block, row_place):
        raw = jnp.einsum("qkgd,skd->kgqs", query_block, key_heads, preferred_element_type=F32)
        return jnp.where(place[None, :] <= row_place[:, None], raw * factor, -1e30)

    attn_parts, log_sums, out_parts = {}, {}, {}
    for j in reversed(range(len(ids))):
        masked = block_scores(q_parts[j], part(place, j))
        row_max = jnp.max(masked, axis=-1, keepdims=True)
        powers = jnp.exp(masked - row_max)
        row_total = jnp.sum(powers, axis=-1, keepdims=True)
        prob_bf = (powers / row_total).astype(BF16)
        log_sums[j] = row_max + jnp.log(row_total)
        attn_parts[j] = (
            jnp.einsum("kgqs,skd->qkgd", prob_bf, value_heads, preferred_element_type=F32)
            .reshape(own_rows, local_heads * HD)
            .astype(BF16)
        )
        out_parts[j] = dot_nn(attn_parts[j], w_output).astype(BF16)
    order = range(len(ids))
    attn_bf = jnp.concatenate([attn_parts[j] for j in order])
    h_one_rows = x_rows + survive * rows.scatter([out_parts[j] for j in order])
    n_two_parts = rows.gather(rms_scale(h_one_rows, gain_mlp).astype(BF16))

    hidden_parts, dgate_parts, dup_parts = [], [], []
    for block, grad_block in zip(n_two_parts, grad_m_parts):
        gate_proj = dot_nn(block, w_gate)
        up_proj = dot_nn(block, w_up)
        sig_gate = jax.nn.sigmoid(gate_proj)
        silu_gate = gate_proj * sig_gate
        hidden_parts.append((silu_gate * up_proj).astype(BF16))
        grad_hidden = dot_nt(grad_block, w_down)
        dgate_parts.append(
            (grad_hidden * up_proj * sig_gate * (1.0 + gate_proj * (1.0 - sig_gate))).astype(BF16)
        )
        dup_parts.append((grad_hidden * silu_gate).astype(BF16))
    hidden = jnp.concatenate(hidden_parts)
    dgate = jnp.concatenate(dgate_parts)
    dup = jnp.concatenate(dup_parts)
    n_two = jnp.concatenate(n_two_parts)
    grad_m = jnp.concatenate(grad_m_parts)
    n_one = jnp.concatenate(n_one_parts)

    grad_n_two_rows = rows.scatter(
        [(dot_nt(a, w_gate) + dot_nt(b, w_up)).astype(BF16) for a, b in zip(dgate_parts, dup_parts)]
    )
    mlp_rows = rows.scatter([dot_nn(a, w_down).astype(BF16) for a in hidden_parts])
    mixed = (h_one_rows + survive * mlp_rows).astype(BF16)[None]

    _, pull_two = jax.vjp(lambda hidden_in: rms_scale(hidden_in, gain_mlp), h_one_rows)
    grad_h_rows = cot_rows + pull_two(grad_n_two_rows)[0]
    gain_two_part = gain_part(h_one_rows, grad_n_two_rows)
    grad_a_parts = rows.gather((survive * grad_h_rows).astype(BF16))
    grad_a = jnp.concatenate(grad_a_parts)
    grad_attn = (
        jnp.concatenate([dot_nt(a, w_output).astype(BF16) for a in grad_a_parts])
    ).reshape(seq_len, local_kv, share, HD)

    query_grads = []
    key_grad = jnp.zeros((seq_len, local_kv, HD), F32)
    value_grad = jnp.zeros((seq_len, local_kv, HD), F32)
    for j in order:
        query_block = q_parts[j]
        masked = block_scores(query_block, part(place, j))
        prob_f32 = jnp.exp(masked - log_sums[j])
        prob_bf = prob_f32.astype(BF16)
        grad_block = part(grad_attn, j)
        grad_prob = jnp.einsum(
            "qkgd,skd->kgqs", grad_block, value_heads, preferred_element_type=F32
        )
        row_delta = jnp.sum(prob_f32 * grad_prob, axis=-1, keepdims=True)
        grad_score = (prob_f32 * (grad_prob - row_delta)).astype(BF16)
        query_grads.append(
            jnp.einsum("kgqs,skd->qkgd", grad_score, key_heads, preferred_element_type=F32)
            * factor
        )
        key_grad = (
            key_grad
            + jnp.einsum("kgqs,qkgd->skd", grad_score, query_block, preferred_element_type=F32)
            * factor
        )
        value_grad = value_grad + jnp.einsum(
            "kgqs,qkgd->skd", prob_bf, grad_block, preferred_element_type=F32
        )
    query_grad = jnp.concatenate(query_grads, axis=0).reshape(seq_len, local_heads, HD)
    grad_q_bf = (
        rotate(query_grad, cos_table, -sin_table).reshape(seq_len, local_heads * HD).astype(BF16)
    )
    grad_k_bf = (
        rotate(key_grad, cos_table, -sin_table).reshape(seq_len, local_kv * HD).astype(BF16)
    )
    grad_v_bf = value_grad.reshape(seq_len, local_kv * HD).astype(BF16)
    grad_n_one = rows.scatter(
        [
            (
                dot_nt(part(grad_q_bf, j), w_query)
                + dot_nt(part(grad_k_bf, j), w_key)
                + dot_nt(part(grad_v_bf, j), w_value)
            ).astype(BF16)
            for j in order
        ]
    )
    _, pull_one = jax.vjp(lambda hidden_in: rms_scale(hidden_in, gain_attn), x_rows)
    input_grad = (grad_h_rows + pull_one(grad_n_one)[0])[None]
    gain_one_part = gain_part(x_rows, grad_n_one)
    gain_sums = psum_small(jnp.stack([gain_one_part, gain_two_part]), mesh_shape)

    down, gate, up, out, query, key, value = sums.run(
        [
            (hidden, grad_m, 1, 4),
            (n_two, dgate, 0, 4),
            (n_two, dup, 0, 4),
            (attn_bf, grad_a, 1, 2),
            (n_one, grad_q_bf, 0, 2),
            (n_one, grad_k_bf, 0, 1),
            (n_one, grad_v_bf, 0, 1),
        ]
    )
    return (
        mixed,
        input_grad,
        query,
        key,
        value,
        out,
        gate,
        up,
        down,
        gain_sums[0],
        gain_sums[1],
    )


def solution(mesh):
    shape = dict(mesh.shape)
    placed = (
        P("dp", "tensor", None),
        P("dp", "tensor", None),
        P(None, "tensor"),
        P(None, "tensor"),
        P(None, "tensor"),
        P("tensor", None),
        P(None, "tensor"),
        P(None, "tensor"),
        P("tensor", None),
        P(),
        P(),
        P("dp"),
        P("dp"),
        P("dp", None),
    )

    def step(*args):
        return local(shape, *args)

    return jax.shard_map(
        step,
        mesh=mesh,
        in_specs=placed,
        out_specs=(
            P("dp", "tensor", None),
            P("dp", "tensor", None),
            P(None, "tensor"),
            P(None, "tensor"),
            P(None, "tensor"),
            P("tensor", None),
            P(None, "tensor"),
            P(None, "tensor"),
            P("tensor", None),
            P(),
            P(),
        ),
        check_vma=False,
    )
```

```python
import functools
import math

import jax
import jax.numpy as jnp
from jax import lax
from jax.experimental import pallas as pl
from jax.experimental.pallas import tpu as pltpu
from jax.sharding import PartitionSpec as P

HD = 128
EPS = 1e-05
F32 = jnp.float32
BF16 = jnp.bfloat16
VMEM = pl.BlockSpec(memory_space=pltpu.VMEM)
SMEM = pl.BlockSpec(memory_space=pltpu.SMEM)
HBM = pl.BlockSpec(memory_space=pltpu.HBM)
PER_US = 1150000000.0
MIB = 1024 * 1024
LIMIT = 28


def spec(shape, dtype=BF16):
    return jax.ShapeDtypeStruct(tuple(shape), dtype)


def mm(a, b, dims):
    return lax.dot_general(a, b, (dims, ((), ())), preferred_element_type=F32)


def nn(a, b):
    return mm(a, b, ((1,), (0,)))


def nt(a, b):
    return mm(a, b, ((1,), (1,)))


def tn(a, b):
    return mm(a, b, ((0,), (0,)))


def stack(refs):
    return jnp.concatenate([r[...] for r in refs], axis=0)


def tiles(total, step):
    return [(at, min(step, total - at)) for at in range(0, total, step)]


def put_rows(refs, value, cols=slice(None)):
    rows = refs[0].shape[0]
    for i, ref in enumerate(refs):
        ref[:, cols] = value[i * rows : (i + 1) * rows].astype(ref.dtype)


def in_hbm(value):
    return pltpu.with_memory_space_constraint(value, pltpu.HBM)


class Order:
    def __init__(self):
        self.last = ()

    def tie(self, *values):
        if not self.last:
            return values if len(values) > 1 else values[0]
        out = lax.optimization_barrier((self.last[0], *values))[1:]
        return out if len(values) > 1 else out[0]

    def call(
        self,
        body,
        operands,
        outs,
        smem=(),
        prefetch=(),
        scratch=(),
        grid=(),
        ins=None,
        outspecs=None,
        reuse=(),
        us=1.5,
    ):
        ahead, total = len(prefetch) + len(smem), len(prefetch) + len(smem) + len(operands)
        skip = len(self.last) + len(reuse)

        def kernel(*refs):
            results = refs[total + skip :]
            body(*refs[:total], *results[: len(outs)], *results[len(outs) + 1 :])

        got = pl.pallas_call(
            kernel,
            out_shape=(*outs, pltpu.HBM((8, 128), F32)),
            grid_spec=pltpu.PrefetchScalarGridSpec(
                num_scalar_prefetch=len(prefetch),
                grid=grid,
                in_specs=[SMEM] * len(smem)
                + list(ins or [VMEM] * len(operands))
                + [HBM] * skip,
                out_specs=(*(outspecs or [VMEM] * len(outs)), HBM),
                scratch_shapes=scratch,
            ),
            input_output_aliases={total + len(self.last) + n: n for n in range(len(reuse))},
            cost_estimate=pl.CostEstimate(
                flops=int(2e10), bytes_accessed=int(1.2e8), transcendentals=0
            ),
            compiler_params=pltpu.CompilerParams(vmem_limit_bytes=LIMIT * MIB),
        )(*prefetch, *smem, *operands, *map(in_hbm, (*self.last, *reuse)))
        self.last = (got[-1],)
        return got[:-1]


def swap(value, axis, size, bit):
    return lax.ppermute(value, axis, [(i, i ^ bit) for i in range(size)])


def row_blocks(arrays, steps):
    return [pl.BlockSpec((a.shape[0] // steps, a.shape[1]), lambda i: (i, 0)) for a in arrays]


def pointwise(order, body, operands, outs, smem=(), steps=1, us=1.5):
    return order.call(
        body,
        operands,
        outs,
        smem=smem,
        grid=(steps,),
        ins=row_blocks(operands, steps),
        outspecs=row_blocks(outs, steps),
        us=us,
    )


def plus(a_ref, b_ref):
    return a_ref[...].astype(F32) + b_ref[...].astype(F32)


def add(order, a, b):
    def body(a_ref, b_ref, out):
        out[...] = plus(a_ref, b_ref).astype(out.dtype)

    return pointwise(order, body, (a, b), [spec(a.shape, a.dtype)])[0]


class Rows:
    def __init__(self, size, own_rows, square):
        self.size = size
        self.square = square
        me = lax.axis_index("tensor")
        if self.square:
            half = own_rows // 2
            where = [(0, 0), (0, 1), (1, 0), (2, 1), (1, 1), (2, 0), (3, 0), (3, 1)]
            self.bases = jnp.stack([(me ^ r) * own_rows + h * half for r, h in where])
            self.piece = half
            self.blocks = [(6, 7), (2, 4), (5, 3), (0, 1)]
        else:
            self.bases = jnp.arange(size, dtype=jnp.int32) * own_rows
            self.piece = own_rows
            self.blocks = [(i, i + 1) for i in range(0, size, 2)]
        self.count = self.bases.shape[0]
        self.groups = [(i, i + 1) for i in range(0, self.count, 2)]
        self.own = [0, 1] if self.square else None

    def swap(self, value, bit):
        return swap(value, "tensor", self.size, bit)

    def gather_first(self, pieces):
        top, low = pieces
        return [top, low, self.swap(top, 1), self.swap(low, 2)]

    def gather_second(self, pieces):
        top, low = pieces
        return [self.swap(low, 1), self.swap(top, 2)]

    def gather_third(self, x_top, y_low):
        return [self.swap(x_top, 2), self.swap(y_low, 1)]

    def gather_all(self, block):
        return lax.all_gather(block, "tensor", axis=0, tiled=True)

    def gather_whole(self, block):
        return jnp.split(self.gather_all(block), self.size, axis=0)

    def scatter_all(self, whole):
        return lax.psum_scatter(whole, "tensor", scatter_dimension=0, tiled=True)

    def scatter_whole(self, pieces):
        return [[self.scatter_all(jnp.concatenate(pieces, axis=0))]]


class Scatter:
    def __init__(self, order, rows):
        self.order, self.rows, self.parts = order, rows, {}

    def far(self, pieces):
        self.parts.update(pieces)
        if self.rows.square:
            self.y_top = self.rows.swap(pieces[6], 1)
            self.x_low = self.rows.swap(pieces[7], 2)

    def near(self, pieces):
        self.parts.update(pieces)
        if self.rows.square:
            self.x_got_top = self.rows.swap(pieces[2], 1)
            self.y_got_low = self.rows.swap(pieces[3], 2)

    def rest(self, pieces):
        self.parts.update(pieces)
        if self.rows.square:
            self.x_got_low = self.rows.swap(add(self.order, pieces[4], self.x_low), 1)
            self.y_got_top = self.rows.swap(add(self.order, pieces[5], self.y_top), 2)

    def own(self, pieces):
        self.parts.update(pieces)

    def result(self):
        if not self.rows.square:
            return self.rows.scatter_whole([self.parts[i] for i in range(self.rows.count)])
        return [
            [self.parts[0], self.parts[1]],
            [self.x_got_top, self.x_got_low],
            [self.y_got_top, self.y_got_low],
        ]


class Pieced:
    def __init__(self, pieces, rows, width, steps=1):
        self.pieces, self.steps, self.width = pieces, steps, width
        self.grid = (pieces, steps)
        self.block = rows // (pieces * steps)
        self.whole = pl.BlockSpec((self.block, width), lambda p, i: (p * steps + i, 0))
        self.row = pl.BlockSpec((1, width), lambda p, i: (0, 0))

    def piece(self, q):
        last = self.steps - 1
        return pl.BlockSpec(
            (self.block, self.width),
            lambda p, i: (jnp.where(p == q, i, jnp.where(p < q, 0, last)), 0),
        )

    def lists(self, count):
        return [self.piece(q) for _ in range(count) for q in range(self.pieces)]

    def each(self, step):
        for q in range(self.pieces):
            pl.when(pl.program_id(0) == q)(lambda q=q: step(q))

    def total(self, refs, q):
        return sum(ref[...].astype(F32) for ref in refs[q :: self.pieces])


def prepare(order, x, ct, gain, scal, pieces):
    rows, width = x.shape
    plan = Pieced(pieces, rows, width)

    def body(s, x_ref, ct_ref, gain_ref, grad, *outs):
        def step(q):
            value = x_ref[...].astype(F32)
            inv = lax.rsqrt(jnp.mean(value * value, axis=1, keepdims=True) + EPS)
            outs[q][...] = (value * inv * gain_ref[...]).astype(BF16)
            grad[...] = (s[0] * (ct_ref[...].astype(F32) * s[1])).astype(BF16)

        plan.each(step)

    grad, *outs = order.call(
        body,
        (x, ct, gain),
        [spec((rows, width))] + [spec((rows // pieces, width))] * pieces,
        smem=(scal,),
        grid=plan.grid,
        ins=[plan.whole, plan.whole, plan.row],
        outspecs=[plan.whole, *plan.lists(1)], us=2.5)
    return outs, grad


def project(order, pieces, weights, tables, bases, which, earlier=None):
    rows = pieces[0].shape[0]
    width, kv = weights[0].shape[1], weights[1].shape[1]
    many = 0 if earlier is None else len(earlier)
    total = tables[0].shape[0]

    def body(base, a_ref, b_ref, wq, wk, wv, cos_ref, sin_ref, *refs):
        olds, outs = refs[: 2 * many], refs[2 * many :]
        block = stack([a_ref, b_ref])
        ats = [pl.ds(pl.multiple_of(base[i], rows), rows) for i in which]
        cos = jnp.concatenate([cos_ref[at, :] for at in ats])
        sin = jnp.concatenate([sin_ref[at, :] for at in ats])

        def turn(value, refs_out):
            for h in range(value.shape[1] // HD):
                cols = slice(h * HD, (h + 1) * HD)
                u = value[:, cols]
                put_rows(refs_out, u * cos + pltpu.roll(u, HD // 2, 1) * sin, cols)

        turn(nn(block, wq[...]), outs[0:2])
        turn(nn(block, wk[...]), outs[2:4])
        put_rows(outs[4:6], nn(block, wv[...]))
        if many:
            k_all, v_all = outs[6:8]
            done = [i for i in range(many + 2) if i not in which]
            for n, i in enumerate(done):
                at = pl.ds(pl.multiple_of(base[i], rows), rows)
                k_all[at, :] = olds[n][...]
                v_all[at, :] = olds[many + n][...]
            for n in range(2):
                k_all[ats[n], :] = outs[2 + n][...]
                v_all[ats[n], :] = outs[4 + n][...]

    outs = [spec((rows, width))] * 2 + [spec((rows, kv))] * 4
    operands = [*pieces, *weights, *tables]
    if many:
        outs += [spec((total, kv))] * 2
        operands += [k for k, _ in earlier] + [v for _, v in earlier]
    return order.call(body, operands, outs, smem=(bases,), us=2.5)


def attend(order, queries, k_all, v_all, w_out, bases, first):
    piece, width = queries[0].shape
    rows = 2 * piece
    heads = width // HD
    share = heads // (k_all.shape[1] // HD)
    factor = 1.0 / math.sqrt(HD)
    wide = w_out.shape[1]
    blocks = k_all.shape[0] // rows

    def body(base, qa, qb, k_ref, v_ref, wo, *outs):
        attn, lses, parts = outs[0:2], outs[2:4], outs[4:6]
        query_all = stack([qa, qb])
        low = lax.broadcasted_iota(jnp.int32, (rows, rows), 1) <= lax.broadcasted_iota(
            jnp.int32, (rows, rows), 0
        )
        place = base[first] // rows

        def upto(n):
            for h in range(heads):
                g = h // share
                cols = slice(h * HD, (h + 1) * HD)
                kv = slice(g * HD, (g + 1) * HD)
                query = query_all[:, cols]
                raw = [nt(query, k_ref[j * rows : (j + 1) * rows, kv]) for j in range(n)]
                raw[-1] = jnp.where(low, raw[-1], -1e30)
                top = functools.reduce(
                    jnp.maximum, [jnp.max(s, axis=1, keepdims=True) for s in raw]
                )
                powers = [jnp.exp((s - top) * factor) for s in raw]
                total = sum(jnp.sum(p, axis=1, keepdims=True) for p in powers)
                mixed = sum(
                    nn(powers[j].astype(BF16), v_ref[j * rows : (j + 1) * rows, kv])
                    for j in range(n)
                )
                put_rows(attn, mixed / total, cols)
                put_rows(lses, top * factor + jnp.log(total), slice(h, h + 1))

        for n in range(1, blocks + 1):
            pl.when(place == n - 1)(functools.partial(upto, n))
        value = stack(attn)
        for at, size in tiles(wide, 512):
            put_rows(parts, nn(value, wo[:, at : at + size]), slice(at, at + size))

    return order.call(
        body,
        (*queries, k_all, v_all, w_out),
        [spec((piece, width))] * 2 + [spec((piece, heads), F32)] * 2 + [spec((piece, wide))] * 2,
        smem=(bases,), us=3.0)


def second_norm(order, x, sums, gain, scal, pieces):
    rows, width = x.shape
    plan = Pieced(pieces, rows, width)
    count = len(sums)

    def body(s, x_ref, gain_ref, *refs):
        h_one, *outs = refs[count * pieces :]

        def step(q):
            value = x_ref[...].astype(F32) + s[0] * plan.total(refs[: count * pieces], q)
            h_one[...] = value
            inv = lax.rsqrt(jnp.mean(value * value, axis=1, keepdims=True) + EPS)
            outs[q][...] = (value * inv * gain_ref[...]).astype(BF16)

        plan.each(step)

    got = order.call(
        body,
        (x, gain, *[p for s in sums for p in s]),
        [spec((rows, width), F32)] + [spec((rows // pieces, width))] * pieces,
        smem=(scal,),
        grid=plan.grid,
        ins=[plan.whole, plan.row, *plan.lists(count)],
        outspecs=[plan.whole, *plan.lists(1)], us=2.4)
    return got[0], list(got[1:])


def put_pieces(out, value, base, piece, cols=slice(None)):
    for p in range(value.shape[0] // piece):
        at = pl.ds(pl.multiple_of(base[p], piece), piece)
        out[at, cols] = value[p * piece : (p + 1) * piece].astype(out.dtype)


def back_hidden(order, grad_m, w_down, step=512):
    rows, depth = grad_m.shape
    width = w_down.shape[0]

    def body(grad_ref, wd, out):
        out[...] = nt(grad_ref[...], wd[...]).astype(BF16)

    return order.call(
        body,
        (grad_m, w_down),
        [spec((rows, width))],
        grid=(pl.cdiv(width, step),),
        ins=[VMEM, pl.BlockSpec((step, depth), lambda i: (i, 0))],
        outspecs=[pl.BlockSpec((rows, step), lambda i: (0, i))], us=7.3)[0]


def feed_forward(order, n_pieces, dhid, w_gate, w_up, bases, which, step=512):
    piece, depth = n_pieces[0].shape
    width = w_gate.shape[1]
    rows = 2 * piece

    def body(base, na, nb, da, db, wg, wu, hid, dg, du):
        n_two = stack([na, nb])
        gate = nn(n_two, wg[...])
        up = nn(n_two, wu[...])
        grad = stack([da, db]).astype(F32)
        sig = 1.0 / (1.0 + jnp.exp(-gate))
        silu = gate * sig
        hid[...] = (silu * up).astype(BF16)
        dg[...] = (grad * up * (sig + silu * (1.0 - sig))).astype(BF16)
        du[...] = (grad * silu).astype(BF16)

    def rows_of(p):
        return pl.BlockSpec((piece, step), lambda i, base: (base[p] // piece, i))

    across = pl.BlockSpec((depth, step), lambda i, base: (0, i))
    out = pl.BlockSpec((rows, step), lambda i, base: (0, i))
    return order.call(
        body,
        (*n_pieces, dhid, dhid, w_gate, w_up),
        [spec((rows, width))] * 3,
        prefetch=(bases,),
        grid=(pl.cdiv(width, step),),
        ins=[VMEM, VMEM, rows_of(which[0]), rows_of(which[1]), across, across],
        outspecs=[out] * 3, us=7.3)


def back_two(order, dgates, dups, w_gate, w_up, bases, piece, step=256):
    many = len(dgates)
    depth, width = w_gate.shape
    rows = many * dgates[0].shape[0]

    def body(base, *refs):
        wg, wu, out = refs[2 * many :]
        value = nt(stack(refs[:many]), wg[...]) + nt(stack(refs[many : 2 * many]), wu[...])
        put_pieces(out, value, base, piece)

    weight = pl.BlockSpec((step, width), lambda i: (i, 0))
    return order.call(
        body,
        (*dgates, *dups, w_gate, w_up),
        [spec((rows, depth))],
        smem=(bases,),
        grid=(depth // step,),
        ins=[VMEM] * (2 * many) + [weight, weight],
        outspecs=[pl.BlockSpec((rows, step), lambda i: (0, i))], us=16.0)[0]


def down_rows(order, hiddens, w_down, bases, piece, step=512):
    many = len(hiddens)
    width, depth = w_down.shape
    rows = many * hiddens[0].shape[0]

    def body(base, *refs):
        wd, out = refs[many:]
        put_pieces(out, nn(stack(refs[:many]), wd[...]), base, piece)

    return order.call(
        body,
        (*hiddens, w_down),
        [spec((rows, depth))],
        smem=(bases,),
        grid=(depth // step,),
        ins=[VMEM] * many + [pl.BlockSpec((width, step), lambda i: (0, i))],
        outspecs=[pl.BlockSpec((rows, step), lambda i: (0, i))], us=8.5)[0]


def norm_back(h, gain, grad):
    inv = lax.rsqrt(jnp.mean(h * h, axis=1, keepdims=True) + EPS)
    scaled = grad * gain
    mean = jnp.mean(h * scaled, axis=1, keepdims=True)
    return inv * (scaled - h * (inv * inv * mean)), jnp.sum(grad * h * inv, axis=0, keepdims=True)


def second_back(order, h_one, ct, total, gain, scal, steps=2):
    rows, width = h_one.shape

    def body(s, h_ref, ct_ref, total_ref, gain_ref, dh, gsum, out):
        @pl.when(pl.program_id(0) == 0)
        def _():
            gsum[...] = jnp.zeros_like(gsum)

        grad, gain_grad = norm_back(h_ref[...], gain_ref[...], total_ref[...].astype(F32))
        value = ct_ref[...].astype(F32) * s[1] + grad
        dh[...] = value
        gsum[...] += gain_grad
        out[...] = (s[0] * value).astype(BF16)

    block = pl.BlockSpec((rows // steps, width), lambda i: (i, 0))
    row = pl.BlockSpec((1, width), lambda i: (0, 0))
    return order.call(
        body,
        (h_one, ct, total, gain),
        [spec((rows, width), F32), spec((1, width), F32), spec((rows, width))],
        smem=(scal,),
        grid=(steps,),
        ins=[block, block, block, row],
        outspecs=[block, row, block], us=2.6)


def first_back(order, x, dh, total, gain, steps=2):
    rows, width = x.shape

    def body(x_ref, dh_ref, total_ref, gain_ref, out, gsum):
        @pl.when(pl.program_id(0) == 0)
        def _():
            gsum[...] = jnp.zeros_like(gsum)

        grad, gain_grad = norm_back(
            x_ref[...].astype(F32), gain_ref[...], total_ref[...].astype(F32)
        )
        out[...] = dh_ref[...] + grad
        gsum[...] += gain_grad

    block = pl.BlockSpec((rows // steps, width), lambda i: (i, 0))
    row = pl.BlockSpec((1, width), lambda i: (0, 0))
    return order.call(
        body,
        (x, dh, total, gain),
        [spec((rows, width), F32), spec((1, width), F32)],
        grid=(steps,),
        ins=[block, block, block, row],
        outspecs=[block, row], us=2.8)


def mix(order, h_one, total, scal):
    def body(s, h_ref, total_ref, out):
        out[...] = (h_ref[...] + s[0] * total_ref[...].astype(F32)).astype(BF16)

    return pointwise(order, body, (h_one, total), [spec(h_one.shape)], smem=(scal,), steps=2)[0]


def back_out(order, grad_a, w_out, steps=2):
    rows, depth = grad_a.shape
    width = w_out.shape[0]

    def body(a_ref, wo, out):
        out[...] = nt(a_ref[...], wo[...]).astype(BF16)

    return order.call(
        body,
        (grad_a, w_out),
        [spec((rows, width))],
        grid=(steps,),
        ins=[pl.BlockSpec((rows // steps, depth), lambda i: (i, 0)), VMEM],
        outspecs=[pl.BlockSpec((rows // steps, width), lambda i: (i, 0))], us=3.0)[0]


def attend_back(order, qs, k_all, v_all, grads, lses, tables, bases):
    count = len(qs)
    piece, width = qs[0].shape
    rows = 2 * piece
    heads = width // HD
    total, kv_width = k_all.shape
    groups = kv_width // HD
    share = heads // groups
    factor = 1.0 / math.sqrt(HD)

    def body(base, *refs):
        q_in, lse_in = refs[:count], refs[count : 2 * count]
        do_ref, k_ref, v_ref, cos_ref, sin_ref, out, q_ref, lse_ref, dq, dk, dv = refs[2 * count :]
        for p in range(count):
            at = pl.ds(pl.multiple_of(base[p], piece), piece)
            q_ref[at, :] = q_in[p][...]
            lse_ref[at, :] = lse_in[p][...]
        low = lax.broadcasted_iota(jnp.int32, (rows, rows), 1) <= lax.broadcasted_iota(
            jnp.int32, (rows, rows), 0
        )
        dk[...] = jnp.zeros_like(dk)
        dv[...] = jnp.zeros_like(dv)
        for i in range(total // rows):
            here = slice(i * rows, (i + 1) * rows)
            for h in range(heads):
                g = h // share
                cols = slice(h * HD, (h + 1) * HD)
                kv = slice(g * HD, (g + 1) * HD)
                query, grad = q_ref[here, cols], do_ref[here, cols]
                lse = lse_ref[here, h : h + 1]
                probs, dps = [], []
                for j in range(i + 1):
                    there = slice(j * rows, (j + 1) * rows)
                    prob = jnp.exp(nt(query, k_ref[there, kv]) * factor - lse)
                    probs.append(jnp.where(low, prob, 0.0) if j == i else prob)
                    dps.append(nt(grad, v_ref[there, kv]))
                delta = sum(
                    jnp.sum(p * d, axis=1, keepdims=True) for p, d in zip(probs, dps)
                )
                sum_q = jnp.zeros((rows, HD), F32)
                for j in range(i + 1):
                    there = slice(j * rows, (j + 1) * rows)
                    ds = (probs[j] * (dps[j] - delta)).astype(BF16)
                    sum_q += nn(ds, k_ref[there, kv])
                    dk[there, kv] += tn(ds, query)
                    dv[there, kv] += tn(probs[j].astype(BF16), grad)
                dq[here, cols] = sum_q
        for p in range(count):
            at = pl.ds(pl.multiple_of(base[p], piece), piece)
            to = slice(p * piece, (p + 1) * piece)
            cos, sin = cos_ref[at, :], sin_ref[at, :]
            for src, wide, start in ((dq, width, 0), (dk, kv_width, width)):
                for h in range(wide // HD):
                    w = src[at, h * HD : (h + 1) * HD] * factor
                    turned = w * cos - pltpu.roll(w, HD // 2, 1) * sin
                    out[to, start + h * HD : start + (h + 1) * HD] = turned.astype(BF16)
            out[to, width + kv_width :] = dv[at, :].astype(BF16)

    return order.call(
        body,
        (*qs, *lses, grads, k_all, v_all, *tables),
        [spec((total, width + 2 * kv_width))],
        smem=(bases,),
        scratch=[
            pltpu.VMEM((total, width), BF16),
            pltpu.VMEM((total, heads), F32),
            pltpu.VMEM((total, width), F32),
            pltpu.VMEM((total, kv_width), F32),
            pltpu.VMEM((total, kv_width), F32),
        ], us=13.8)[0]


def back_one(order, grads, weights, bases, piece, step=512):
    rows, total = grads.shape
    depth = weights[0].shape[0]
    edges = [0]
    for w in weights:
        edges.append(edges[-1] + w.shape[1])

    def body(base, g_ref, *refs):
        value = sum(
            nt(g_ref[:, edges[i] : edges[i + 1]], refs[i][...]) for i in range(len(weights))
        )
        put_pieces(refs[-1], value, base, piece)

    return order.call(
        body,
        (grads, *weights),
        [spec((rows, depth))],
        smem=(bases,),
        grid=(depth // step,),
        ins=[VMEM] + [pl.BlockSpec((step, w.shape[1]), lambda i: (i, 0)) for w in weights],
        outspecs=[pl.BlockSpec((rows, step), lambda i: (0, i))], us=6.0)[0]


class Job:
    def __init__(self, groups, outs, half=256):
        self.groups, self.outs, self.half = groups, outs, half
        self.pairs = [pair for group in groups for pair in group]
        self.rows = self.pairs[0][0][0].shape[1]
        self.chunks = self.rows // (2 * half)
        self.widths = [sum(right[0].shape[1] for _, right, _ in group) for group in groups]
        self.results = [() for _ in groups]
        self.got = {}


def product(order, job, pick, chunks, bases, piece, add_to=None):
    first, count, half, many = chunks[0], len(chunks), job.half, len(job.groups)
    width = job.widths[0]
    lefts, places = [], []
    for left, _, _ in job.pairs:
        if not any(left is known for known, _ in places):
            places.append((left, len(lefts)))
            lefts += left
    rights = [block for _, right, _ in job.pairs for block in right]
    total = sum(p.shape[0] for p in job.pairs[0][0])
    extra = 0 if add_to is None else 1

    def body(pick_ref, base, *refs):
        left_refs, refs = refs[: len(lefts)], refs[len(lefts) :]
        right_refs, refs = refs[: len(rights)], refs[len(rights) :]
        got, outs, whole = refs[:extra], refs[extra:-1], refs[-1]

        @pl.when(pl.program_id(0) == 0)
        def _():
            at, n = 0, 0
            for _, right, placed in job.pairs:
                wide = right[0].shape[1]
                value = stack(right_refs[n : n + len(right)])
                here = slice(at, at + wide)
                if placed:
                    put_pieces(whole, value, base, piece, here)
                else:
                    whole[:, here] = value
                at += wide
                n += len(right)

        stacks = {
            start: stack(left_refs[start : start + len(left)]) for left, start in places
        }
        at = 0
        for g, group in enumerate(job.groups):
            put = 0
            for left, right, _ in group:
                wide = right[0].shape[1]
                start = next(s for known, s in places if known is left)
                value = tn(stacks[start], whole[:, at : at + wide])
                here = slice(put, put + wide)
                if extra:
                    mine = slice(g * half, (g + 1) * half)
                    value = (value + got[0][mine, here].astype(F32)).astype(BF16)
                    for i in range(count):

                        @pl.when(pl.program_id(0) == i)
                        def _():
                            outs[i * many + g][:, here] = value
                else:
                    outs[0][g * half : (g + 1) * half, here] = value.astype(BF16)
                at += wide
                put += wide

    block = pl.BlockSpec((many * half, width), lambda i, pick_ref, base: (i, 0))
    if extra:
        outs, outspecs = [spec((half, width))] * (count * many), None
    else:
        outs, outspecs = [spec((count * many * half, width))], [block]
    return order.call(
        body,
        (*lefts, *rights, *([add_to] if extra else [])),
        outs,
        prefetch=(pick, bases),
        grid=(count,),
        ins=[
            pl.BlockSpec((p.shape[0], half), lambda i, pick_ref, base: (0, 2 * (first + i) + pick_ref[0]))
            for p in lefts
        ]
        + [VMEM] * len(rights)
        + [block] * extra,
        outspecs=outspecs,
        scratch=[pltpu.VMEM((total, sum(job.widths)), BF16)], us=0.5 + count * many * half * width / 2.4e5)


def lay(order, job, group, core, chunk, mine, other):
    block = job.half

    def body(core_ref, mine_ref, other_ref, *outs):
        for n, ref in ((0, mine_ref), (1, other_ref)):

            @pl.when(pl.program_id(0) == n)
            def _():
                for (at, width, turned), out in zip(job.outs[group], outs):
                    value = ref[:, at : at + width].astype(F32)
                    out[...] = value.T if turned else value

    def place(n, core_ref):
        return 2 * chunk + (core_ref[0] ^ n)

    def across(n, core_ref):
        return (place(n, core_ref), 0)

    def down(n, core_ref):
        return (0, place(n, core_ref))

    shapes, specs = [], []
    for _, width, turned in job.outs[group]:
        shapes.append(pltpu.HBM((width, job.rows) if turned else (job.rows, width), F32))
        specs.append(
            pl.BlockSpec((width, block), down) if turned else pl.BlockSpec((block, width), across)
        )
    job.results[group] = order.call(
        body,
        (mine, other),
        shapes,
        prefetch=(core,),
        grid=(2,),
        outspecs=specs,
        reuse=job.results[group], us=2.5)


class Line:
    LAG = 2

    def __init__(self, order, size, bases, piece):
        self.order, self.size, self.bases, self.piece = order, size, bases, piece
        where = lax.axis_index("dp")
        core, z = where % 2, where // 2
        self.mine = core.reshape(1).astype(jnp.int32)
        self.other = (1 - core).reshape(1).astype(jnp.int32)
        self.middle = ((z == 1) | (z == 2)).astype(jnp.int32).reshape(1)
        self.count = 0
        self.chunks = []
        self.part, self.fold, self.half, self.mids = [], {}, {}, {}
        self.whole, self.ends, self.final, self.done = {}, {}, {}, {}

    def hop(self, value, steps):
        pairs = [(2 * a + c, 2 * b + c) for a, b in steps for c in range(2)]
        return lax.ppermute(value, "dp", pairs)

    def send(self, job, chunks):
        part = product(self.order, job, self.other, chunks, self.bases, self.piece)[0]
        job.got[tuple(chunks)] = swap(part, "dp", self.size, 1)

    def enter(self, job, chunks):
        got = job.got[tuple(chunks)]
        parts = iter(product(self.order, job, self.mine, chunks, self.bases, self.piece, got))
        for k in chunks:
            for group in range(len(job.groups)):
                part = next(parts)
                n = len(self.part)
                if n < 2 * self.LAG:
                    self.fold[n] = self.hop(part, [(0, 1), (3, 2)])
                self.chunks.append((job, group, k))
                self.part.append(part)

    def tick(self, k):
        b, c, ahead = k - self.LAG, k - 2 * self.LAG, k + self.LAG
        here, back, out = k < self.count, 0 <= b < self.count, 0 <= c < self.count
        on = 2 * self.LAG <= ahead < self.count
        merged = back and on and self.half[b].shape == self.part[ahead].shape
        operands, outs = [], []
        if here:
            operands += [self.part[k], self.fold[k]]
            outs.append(spec(self.part[k].shape))
        if back:
            operands += [self.half[b], self.mids[b]]
            outs.append(spec(self.half[b].shape))
        if merged:
            operands.append(self.part[ahead])
        if out:
            operands += [self.whole[c], self.ends[c]]
            outs.append(spec(self.whole[c].shape))

        def body(flag, *refs):
            middle = flag[0] != 0
            refs, results = list(refs[: len(operands)]), list(refs[len(operands) :])
            if here:
                results.pop(0)[...] = plus(refs.pop(0), refs.pop(0)).astype(BF16)
            if back:
                both = plus(refs.pop(0), refs.pop(0)).astype(BF16)
                results.pop(0)[...] = jnp.where(middle, both, refs.pop(0)[...]) if merged else both
            if out:
                results.pop(0)[...] = jnp.where(middle, refs.pop(0)[...], refs.pop(0)[...])

        got = list(pointwise(self.order, body, operands, outs, smem=(self.middle,), us=2.5))
        if here:
            self.half[k] = got.pop(0)
        if back:
            self.whole[b] = got.pop(0)
        if out:
            self.final[c] = got.pop(0)
        if here:
            self.mids[k] = self.hop(self.half[k], [(1, 2), (2, 1), (0, 0), (3, 3)])
        if merged:
            both = self.hop(self.whole[b], [(0, 1), (1, 0), (2, 3), (3, 2)])
            self.ends[b] = self.fold[ahead] = both
        else:
            if back:
                self.ends[b] = self.hop(self.whole[b], [(1, 0), (2, 3)])
            if on:
                self.fold[ahead] = self.hop(self.part[ahead], [(0, 1), (3, 2)])
        if out:
            self.done[c] = swap(self.final[c], "dp", self.size, 1)

    def lay(self, i):
        if 0 <= i < self.count:
            job, group, k = self.chunks[i]
            lay(self.order, job, group, self.mine, k, self.final[i], self.done[i])


class SmallSum:
    def __init__(self, order, value, mesh_shape):
        self.order, self.value = order, value
        self.steps = []
        for axis in ("dp", "tensor"):
            size, bit = mesh_shape[axis], 1
            if size & (size - 1):
                self.steps.append((axis, size, None))
                continue
            while bit < size:
                self.steps.append((axis, size, bit))
                bit *= 2

    def step(self):
        if self.steps:
            axis, size, bit = self.steps.pop(0)
            if bit is None:
                self.value = lax.psum(self.value, axis)
            else:
                self.value = add(self.order, self.value, swap(self.value, axis, size, bit))


def local(
    mesh_shape,
    tokens,
    cotangent,
    w_query,
    w_key,
    w_value,
    w_output,
    w_gate,
    w_up,
    w_down,
    gain_attn,
    gain_mlp,
    dropped,
    exit_scale,
    positions,
):
    x, ct = tokens[0], cotangent[0]
    order = Order()
    square = mesh_shape["tensor"] == 4 and mesh_shape["dp"] == 8
    rows = Rows(mesh_shape["tensor"], x.shape[0], square)
    bases = rows.bases
    line = Line(order, mesh_shape["dp"], bases, rows.piece)
    pieces = 2 if square else 1
    scal = jnp.stack([1.0 - dropped[0].astype(F32), exit_scale[0]])
    gain_one, gain_two = gain_attn[None], gain_mlp[None]
    attn_weights = (w_query, w_key, w_value)

    freqs = jnp.exp(jnp.arange(HD // 2, dtype=F32) * (-2.0 * math.log(10000.0) / HD))
    turned = positions[0].astype(F32)[:, None] * freqs[None, :]
    cos, sin = jnp.cos(turned), jnp.sin(turned)
    tables = (jnp.concatenate([cos, cos], axis=1), jnp.concatenate([-sin, sin], axis=1))

    n_own, grad_m_own = prepare(order, x, ct, gain_one, scal, pieces)
    qs, ks, vs = {}, {}, {}

    def project_group(group, n_one):
        last = group is rows.groups[-1]
        done = [(ks[i], vs[i]) for i in sorted(ks)] if last else None
        got = project(
            order, [n_one[i] for i in group], attn_weights, tables, bases, group, done
        )
        for n, i in enumerate(group):
            qs[i], ks[i], vs[i] = got[n], got[2 + n], got[4 + n]
        return got[6:]

    if square:
        n_one = rows.gather_first(n_own)
        n_one += rows.gather_second(n_own)
        project_group(rows.groups[0], n_one)
        n_one += rows.gather_third(*order.tie(n_one[2], n_one[3]))
        project_group(rows.groups[1], n_one)
        project_group(rows.groups[2], n_one)
        grad_m = rows.gather_all(order.tie(grad_m_own))
        k_all, v_all = project_group(rows.groups[3], n_one)
    else:
        n_one = rows.gather_whole(n_own[0])
        grad_m = rows.gather_all(grad_m_own)
        for group in rows.groups:
            k_all, v_all = project_group(group, n_one) or (None, None)

    attn, lses, parts = {}, {}, {}

    def attend_block(block):
        got = attend(order, [qs[i] for i in block], k_all, v_all, w_output, bases, block[0])
        for n, i in enumerate(block):
            attn[i], lses[i], parts[i] = got[n], got[2 + n], got[4 + n]

    out_sum = Scatter(order, rows)
    if square:
        attend_block(rows.blocks[0])
        out_sum.far({i: parts[i] for i in (6, 7)})
        attend_block(rows.blocks[1])
        attend_block(rows.blocks[2])
        out_sum.near({i: parts[i] for i in (2, 3)})
        out_sum.rest({i: parts[i] for i in (4, 5)})
        attend_block(rows.blocks[3])
        out_sum.own({i: parts[i] for i in (0, 1)})
    else:
        for block in rows.blocks:
            attend_block(block)
        out_sum.own(parts)
    h_one, n_two_own = second_norm(order, x, out_sum.result(), gain_two, scal, pieces)

    hidden, dgate, dup = [], [], []
    dhid = back_hidden(order, grad_m, w_down)

    def feed(g):
        group = rows.groups[g]
        got = feed_forward(
            order, [n_two[i] for i in group], dhid, w_gate, w_up, bases, group
        )
        for made, values in zip(got, (hidden, dgate, dup)):
            values.append(made)

    every = range(rows.count)
    if square:
        n_two = rows.gather_first(n_two_own)
        n_two += rows.gather_second(n_two_own)
        feed(0)
        n_two += rows.gather_third(*order.tie(n_two[2], n_two[3]))
        feed(1)
        feed(2)
        feed(3)
    else:
        n_two = rows.gather_whole(n_two_own[0])
        for g in range(len(rows.groups)):
            feed(g)

    def back_two_all():
        return rows.scatter_all(
            back_two(order, dgate, dup, w_gate, w_up, bases, rows.piece)
        )

    def second_back_all(total):
        return second_back(order, h_one, ct, total, gain_two, scal)

    def attend_back_all(grad_a):
        return attend_back(
            order,
            [qs[i] for i in every],
            k_all,
            v_all,
            back_out(order, grad_a, w_output),
            [lses[i] for i in every],
            tables,
            bases,
        )

    def back_one_all(gqkv):
        return rows.scatter_all(back_one(order, gqkv, attn_weights, bases, rows.piece))

    def down_all():
        return rows.scatter_all(down_rows(order, hidden, w_down, bases, rows.piece))

    ff, width, kv = w_gate.shape[1], w_query.shape[1], w_key.shape[1]
    late_outs = [
        (0, width, True),
        (width, width, False),
        (2 * width, kv, False),
        (2 * width + kv, kv, False),
    ]
    down = Job([[([grad_m], hidden, True)]], [[(0, ff, True)]])
    wide = Job(
        [[(n_two, dgate, False)], [(n_two, dup, False)]], [[(0, ff, False)], [(0, ff, False)]]
    )

    def late_job(grad_a, gqkv):
        every_attn = [attn[i] for i in every]
        return Job([[([grad_a], every_attn, True), (n_one, [gqkv], False)]], [late_outs])

    if square:
        line.count = 16
        line.send(down, [0, 1])
        line.send(down, [2, 3])
        line.enter(down, [0, 1])
        two_total = back_two_all()
        line.tick(0)
        line.enter(down, [2, 3])
        line.send(wide, [0, 1])
        line.tick(1)
        line.enter(wide, [0, 1])
        line.tick(2)
        line.send(wide, [2, 3])
        line.tick(3)
        dh, gain_two_sum, grad_a_own = second_back_all(two_total)
        grad_a = rows.gather_all(grad_a_own)
        line.tick(4)
        line.enter(wide, [2, 3])
        line.tick(5)
        line.lay(0)
        mix_total = down_all()
        line.tick(6)
        line.lay(1)
        line.tick(7)
        line.lay(2)
        gqkv = attend_back_all(grad_a)
        late = late_job(grad_a, gqkv)
        line.tick(8)
        line.lay(3)
        line.send(late, [0, 1, 2, 3])
        one_total = back_one_all(gqkv)
        line.tick(9)
        line.lay(4)
        line.enter(late, [0, 1, 2, 3])
        line.tick(10)
        line.lay(5)
        line.tick(11)
        line.lay(6)
        mixed = mix(order, h_one, mix_total, scal)
        line.tick(12)
        line.lay(7)
        line.tick(13)
        line.lay(8)
        input_grad, gain_one_sum = first_back(order, x, dh, one_total, gain_one)
        gains = SmallSum(order, jnp.concatenate([gain_one_sum, gain_two_sum]), mesh_shape)
        for k in range(14, line.count + 2 * line.LAG):
            line.tick(k)
            line.lay(k - 5)
            gains.step()
        line.lay(line.count - 1)
    else:
        dh, gain_two_sum, grad_a_own = second_back_all(back_two_all())
        grad_a = rows.gather_all(grad_a_own)
        gqkv = attend_back_all(grad_a)
        late = late_job(grad_a, gqkv)
        mixed = mix(order, h_one, down_all(), scal)
        input_grad, gain_one_sum = first_back(order, x, dh, back_one_all(gqkv), gain_one)
        gains = SmallSum(order, jnp.concatenate([gain_one_sum, gain_two_sum]), mesh_shape)
        for job in (down, wide, late):
            for n, group in enumerate(job.groups):
                parts = [tn(jnp.concatenate(a), jnp.concatenate(b)) for a, b, _ in group]
                whole = jnp.concatenate(parts, axis=1).astype(BF16)
                whole = lax.psum(whole, "dp").astype(F32)
                job.results[n] = [
                    whole[:, at : at + size].T if turned else whole[:, at : at + size]
                    for at, size, turned in job.outs[n]
                ]
    while gains.steps:
        gains.step()
    grad_output, grad_query, grad_key, grad_value = late.results[0]
    return (
        mixed[None],
        input_grad[None],
        grad_query,
        grad_key,
        grad_value,
        grad_output,
        wide.results[0][0],
        wide.results[1][0],
        down.results[0][0],
        gains.value[0],
        gains.value[1],
    )


def solution(mesh):
    shape = dict(mesh.shape)
    placed = (
        P("dp", "tensor", None),
        P("dp", "tensor", None),
        P(None, "tensor"),
        P(None, "tensor"),
        P(None, "tensor"),
        P("tensor", None),
        P(None, "tensor"),
        P(None, "tensor"),
        P("tensor", None),
        P(),
        P(),
        P("dp"),
        P("dp"),
        P("dp", None),
    )

    def step(*args):
        return local(shape, *args)

    return jax.shard_map(
        step,
        mesh=mesh,
        in_specs=placed,
        out_specs=(
            P("dp", "tensor", None),
            P("dp", "tensor", None),
            P(None, "tensor"),
            P(None, "tensor"),
            P(None, "tensor"),
            P("tensor", None),
            P(None, "tensor"),
            P(None, "tensor"),
            P("tensor", None),
            P(),
            P(),
        ),
        check_vma=False,
    )
```

```python
import functools
import math

import jax
import jax.numpy as jnp
from jax import lax
from jax.experimental import pallas as pl
from jax.experimental.pallas import tpu as pltpu
from jax.sharding import PartitionSpec as P

HD = 128
EPS = 1e-05
F32 = jnp.float32
BF16 = jnp.bfloat16
VMEM = pl.BlockSpec(memory_space=pltpu.VMEM)
SMEM = pl.BlockSpec(memory_space=pltpu.SMEM)
HBM = pl.BlockSpec(memory_space=pltpu.HBM)
STEP_FLOPS, STEP_BYTES = 20_000_000_000, 120_000_000
MIB = 1024 * 1024
LIMIT = 28


def spec(shape, dtype=BF16):
    return jax.ShapeDtypeStruct(tuple(shape), dtype)


def mm(a, b, dims):
    return lax.dot_general(a, b, (dims, ((), ())), preferred_element_type=F32)


def nn(a, b):
    return mm(a, b, ((1,), (0,)))


def nt(a, b):
    return mm(a, b, ((1,), (1,)))


def tn(a, b):
    return mm(a, b, ((0,), (0,)))


def stack(refs):
    return jnp.concatenate([r[...] for r in refs], axis=0)


def tiles(total, step):
    return [(at, min(step, total - at)) for at in range(0, total, step)]


def put_rows(refs, value, cols=slice(None)):
    rows = refs[0].shape[0]
    for i, ref in enumerate(refs):
        ref[:, cols] = value[i * rows : (i + 1) * rows].astype(ref.dtype)


def in_hbm(value):
    return pltpu.with_memory_space_constraint(value, pltpu.HBM)


class Order:
    def __init__(self):
        self.last = ()

    def tie(self, *values):
        if not self.last:
            return values if len(values) > 1 else values[0]
        out = lax.optimization_barrier((self.last[0], *values))[1:]
        return out if len(values) > 1 else out[0]

    def call(
        self,
        body,
        operands,
        outs,
        smem=(),
        prefetch=(),
        scratch=(),
        grid=(),
        ins=None,
        outspecs=None,
        reuse=(),
        wait=(),
        weight=1,
    ):
        ahead, total = len(prefetch) + len(smem), len(prefetch) + len(smem) + len(operands)
        last = (*self.last, *wait)
        skip = len(last) + len(reuse)

        def kernel(*refs):
            results = refs[total + skip :]
            body(*refs[:total], *results[: len(outs)], *results[len(outs) + 1 :])

        got = pl.pallas_call(
            kernel,
            out_shape=(*outs, pltpu.HBM((8, 128), F32)),
            grid_spec=pltpu.PrefetchScalarGridSpec(
                num_scalar_prefetch=len(prefetch),
                grid=grid,
                in_specs=[SMEM] * len(smem)
                + list(ins or [VMEM] * len(operands))
                + [HBM] * skip,
                out_specs=(*(outspecs or [VMEM] * len(outs)), HBM),
                scratch_shapes=scratch,
            ),
            input_output_aliases={total + len(last) + n: n for n in range(len(reuse))},
            cost_estimate=pl.CostEstimate(
                flops=weight * STEP_FLOPS, bytes_accessed=weight * STEP_BYTES, transcendentals=0
            ),
            compiler_params=pltpu.CompilerParams(vmem_limit_bytes=LIMIT * MIB),
        )(*prefetch, *smem, *operands, *map(in_hbm, (*last, *reuse)))
        self.last = (got[-1],)
        return got[:-1]


def swap(value, axis, size, bit):
    return lax.ppermute(value, axis, [(i, i ^ bit) for i in range(size)])


def row_blocks(arrays, steps):
    return [pl.BlockSpec((a.shape[0] // steps, a.shape[1]), lambda i: (i, 0)) for a in arrays]


def pointwise(order, body, operands, outs, smem=(), steps=1, wait=()):
    return order.call(
        body,
        operands,
        outs,
        smem=smem,
        grid=(steps,),
        ins=row_blocks(operands, steps),
        outspecs=row_blocks(outs, steps),
        wait=wait,
    )


def plus(a_ref, b_ref):
    return a_ref[...].astype(F32) + b_ref[...].astype(F32)


def add(order, a, b):
    def body(a_ref, b_ref, out):
        out[...] = plus(a_ref, b_ref).astype(out.dtype)

    return pointwise(order, body, (a, b), [spec(a.shape, a.dtype)])[0]


class Rows:
    def __init__(self, size, own_rows, square):
        self.size = size
        self.square = square
        me = lax.axis_index("tensor")
        if self.square:
            half = own_rows // 2
            where = [(0, 0), (0, 1), (1, 0), (2, 1), (1, 1), (2, 0), (3, 0), (3, 1)]
            self.bases = jnp.stack([(me ^ r) * own_rows + h * half for r, h in where])
            self.piece = half
            self.blocks = [(6, 7), (2, 4), (5, 3), (0, 1)]
        else:
            self.bases = jnp.arange(size, dtype=jnp.int32) * own_rows
            self.piece = own_rows
            self.blocks = [(i, i + 1) for i in range(0, size, 2)]
        self.count = self.bases.shape[0]
        self.groups = [(i, i + 1) for i in range(0, self.count, 2)]
        self.own = [0, 1] if self.square else None

    def swap(self, value, bit):
        return swap(value, "tensor", self.size, bit)

    def gather_first(self, pieces):
        top, low = pieces
        return [top, low, self.swap(top, 1), self.swap(low, 2)]

    def gather_second(self, pieces):
        top, low = pieces
        return [self.swap(low, 1), self.swap(top, 2)]

    def gather_third(self, x_top, y_low):
        return [self.swap(x_top, 2), self.swap(y_low, 1)]

    def gather_all(self, block):
        return lax.all_gather(block, "tensor", axis=0, tiled=True)

    def gather_whole(self, block):
        return jnp.split(self.gather_all(block), self.size, axis=0)

    def scatter_all(self, whole):
        return lax.psum_scatter(whole, "tensor", scatter_dimension=0, tiled=True)

    def scatter_whole(self, pieces):
        return [[self.scatter_all(jnp.concatenate(pieces, axis=0))]]


class Scatter:
    def __init__(self, order, rows):
        self.order, self.rows, self.parts = order, rows, {}

    def far(self, pieces):
        self.parts.update(pieces)
        if self.rows.square:
            self.y_top = self.rows.swap(pieces[6], 1)
            self.x_low = self.rows.swap(pieces[7], 2)

    def near(self, pieces):
        self.parts.update(pieces)
        if self.rows.square:
            self.x_got_top = self.rows.swap(pieces[2], 1)
            self.y_got_low = self.rows.swap(pieces[3], 2)

    def rest(self, pieces):
        self.parts.update(pieces)
        if self.rows.square:
            self.x_got_low = self.rows.swap(add(self.order, pieces[4], self.x_low), 1)
            self.y_got_top = self.rows.swap(add(self.order, pieces[5], self.y_top), 2)

    def own(self, pieces):
        self.parts.update(pieces)

    def result(self):
        if not self.rows.square:
            return self.rows.scatter_whole([self.parts[i] for i in range(self.rows.count)])
        return [
            [self.parts[0], self.parts[1]],
            [self.x_got_top, self.x_got_low],
            [self.y_got_top, self.y_got_low],
        ]


class Pieced:
    def __init__(self, pieces, rows, width, steps=1):
        self.pieces, self.steps, self.width = pieces, steps, width
        self.grid = (pieces, steps)
        self.block = rows // (pieces * steps)
        self.whole = pl.BlockSpec((self.block, width), lambda p, i: (p * steps + i, 0))
        self.row = pl.BlockSpec((1, width), lambda p, i: (0, 0))

    def piece(self, q):
        last = self.steps - 1
        return pl.BlockSpec(
            (self.block, self.width),
            lambda p, i: (jnp.where(p == q, i, jnp.where(p < q, 0, last)), 0),
        )

    def lists(self, count):
        return [self.piece(q) for _ in range(count) for q in range(self.pieces)]

    def each(self, step):
        for q in range(self.pieces):
            pl.when(pl.program_id(0) == q)(lambda q=q: step(q))

    def total(self, refs, q):
        return sum(ref[...].astype(F32) for ref in refs[q :: self.pieces])


def prepare(order, x, ct, gain, scal, pieces):
    rows, width = x.shape
    plan = Pieced(pieces, rows, width)

    def body(s, x_ref, ct_ref, gain_ref, grad, *outs):
        def step(q):
            value = x_ref[...].astype(F32)
            inv = lax.rsqrt(jnp.mean(value * value, axis=1, keepdims=True) + EPS)
            outs[q][...] = (value * inv * gain_ref[...]).astype(BF16)
            grad[...] = (s[0] * (ct_ref[...].astype(F32) * s[1])).astype(BF16)

        plan.each(step)

    grad, *outs = order.call(
        body,
        (x, ct, gain),
        [spec((rows, width))] + [spec((rows // pieces, width))] * pieces,
        smem=(scal,),
        grid=plan.grid,
        ins=[plan.whole, plan.whole, plan.row],
        outspecs=[plan.whole, *plan.lists(1)],
    )
    return outs, grad


def project(order, pieces, weights, tables, bases, which, earlier=None):
    rows = pieces[0].shape[0]
    width, kv = weights[0].shape[1], weights[1].shape[1]
    many = 0 if earlier is None else len(earlier)
    total = tables[0].shape[0]

    def body(base, a_ref, b_ref, wq, wk, wv, cos_ref, sin_ref, *refs):
        olds, outs = refs[: 2 * many], refs[2 * many :]
        block = stack([a_ref, b_ref])
        ats = [pl.ds(pl.multiple_of(base[i], rows), rows) for i in which]
        cos = jnp.concatenate([cos_ref[at, :] for at in ats])
        sin = jnp.concatenate([sin_ref[at, :] for at in ats])

        def turn(value, refs_out):
            for h in range(value.shape[1] // HD):
                cols = slice(h * HD, (h + 1) * HD)
                u = value[:, cols]
                put_rows(refs_out, u * cos + pltpu.roll(u, HD // 2, 1) * sin, cols)

        turn(nn(block, wq[...]), outs[0:2])
        turn(nn(block, wk[...]), outs[2:4])
        put_rows(outs[4:6], nn(block, wv[...]))
        if many:
            k_all, v_all = outs[6:8]
            done = [i for i in range(many + 2) if i not in which]
            for n, i in enumerate(done):
                at = pl.ds(pl.multiple_of(base[i], rows), rows)
                k_all[at, :] = olds[n][...]
                v_all[at, :] = olds[many + n][...]
            for n in range(2):
                k_all[ats[n], :] = outs[2 + n][...]
                v_all[ats[n], :] = outs[4 + n][...]

    outs = [spec((rows, width))] * 2 + [spec((rows, kv))] * 4
    operands = [*pieces, *weights, *tables]
    if many:
        outs += [spec((total, kv))] * 2
        operands += [k for k, _ in earlier] + [v for _, v in earlier]
    return order.call(body, operands, outs, smem=(bases,))


def attend(order, queries, k_all, v_all, w_out, bases, first):
    piece, width = queries[0].shape
    rows = 2 * piece
    heads = width // HD
    share = heads // (k_all.shape[1] // HD)
    factor = 1.0 / math.sqrt(HD)
    wide = w_out.shape[1]
    blocks = k_all.shape[0] // rows

    def body(base, qa, qb, k_ref, v_ref, wo, *outs):
        attn, lses, parts = outs[0:2], outs[2:4], outs[4:6]
        query_all = stack([qa, qb])
        low = lax.broadcasted_iota(jnp.int32, (rows, rows), 1) <= lax.broadcasted_iota(
            jnp.int32, (rows, rows), 0
        )
        place = base[first] // rows

        def upto(n):
            for h in range(heads):
                g = h // share
                cols = slice(h * HD, (h + 1) * HD)
                kv = slice(g * HD, (g + 1) * HD)
                query = query_all[:, cols]
                raw = [nt(query, k_ref[j * rows : (j + 1) * rows, kv]) for j in range(n)]
                raw[-1] = jnp.where(low, raw[-1], -1e30)
                top = functools.reduce(
                    jnp.maximum, [jnp.max(s, axis=1, keepdims=True) for s in raw]
                )
                powers = [jnp.exp((s - top) * factor) for s in raw]
                total = sum(jnp.sum(p, axis=1, keepdims=True) for p in powers)
                mixed = sum(
                    nn(powers[j].astype(BF16), v_ref[j * rows : (j + 1) * rows, kv])
                    for j in range(n)
                )
                put_rows(attn, mixed / total, cols)
                put_rows(lses, top * factor + jnp.log(total), slice(h, h + 1))

        for n in range(1, blocks + 1):
            pl.when(place == n - 1)(functools.partial(upto, n))
        value = stack(attn)
        for at, size in tiles(wide, 512):
            put_rows(parts, nn(value, wo[:, at : at + size]), slice(at, at + size))

    return order.call(
        body,
        (*queries, k_all, v_all, w_out),
        [spec((piece, width))] * 2 + [spec((piece, heads), F32)] * 2 + [spec((piece, wide))] * 2,
        smem=(bases,),
    )


def second_norm(order, x, sums, gain, scal, pieces):
    rows, width = x.shape
    plan = Pieced(pieces, rows, width)
    count = len(sums)

    def body(s, x_ref, gain_ref, *refs):
        h_one, *outs = refs[count * pieces :]

        def step(q):
            value = x_ref[...].astype(F32) + s[0] * plan.total(refs[: count * pieces], q)
            h_one[...] = value
            inv = lax.rsqrt(jnp.mean(value * value, axis=1, keepdims=True) + EPS)
            outs[q][...] = (value * inv * gain_ref[...]).astype(BF16)

        plan.each(step)

    got = order.call(
        body,
        (x, gain, *[p for s in sums for p in s]),
        [spec((rows, width), F32)] + [spec((rows // pieces, width))] * pieces,
        smem=(scal,),
        grid=plan.grid,
        ins=[plan.whole, plan.row, *plan.lists(count)],
        outspecs=[plan.whole, *plan.lists(1)],
    )
    return got[0], list(got[1:])


def put_pieces(out, value, base, piece, cols=slice(None)):
    for p in range(value.shape[0] // piece):
        at = pl.ds(pl.multiple_of(base[p], piece), piece)
        out[at, cols] = value[p * piece : (p + 1) * piece].astype(out.dtype)


def back_hidden(order, grad_m, w_down, step=512):
    rows, depth = grad_m.shape
    width = w_down.shape[0]

    def body(grad_ref, wd, out):
        out[...] = nt(grad_ref[...], wd[...]).astype(BF16)

    return order.call(
        body,
        (grad_m, w_down),
        [spec((rows, width))],
        grid=(pl.cdiv(width, step),),
        ins=[VMEM, pl.BlockSpec((step, depth), lambda i: (i, 0))],
        outspecs=[pl.BlockSpec((rows, step), lambda i: (0, i))],
    )[0]


def feed_forward(order, n_pieces, dhid, w_gate, w_up, bases, which, step=512):
    piece, depth = n_pieces[0].shape
    width = w_gate.shape[1]
    rows = 2 * piece

    def body(base, na, nb, da, db, wg, wu, hid, dg, du):
        n_two = stack([na, nb])
        gate = nn(n_two, wg[...])
        up = nn(n_two, wu[...])
        grad = stack([da, db]).astype(F32)
        sig = 1.0 / (1.0 + jnp.exp(-gate))
        silu = gate * sig
        hid[...] = (silu * up).astype(BF16)
        dg[...] = (grad * up * (sig + silu * (1.0 - sig))).astype(BF16)
        du[...] = (grad * silu).astype(BF16)

    def rows_of(p):
        return pl.BlockSpec((piece, step), lambda i, base: (base[p] // piece, i))

    across = pl.BlockSpec((depth, step), lambda i, base: (0, i))
    out = pl.BlockSpec((rows, step), lambda i, base: (0, i))
    return order.call(
        body,
        (*n_pieces, dhid, dhid, w_gate, w_up),
        [spec((rows, width))] * 3,
        prefetch=(bases,),
        grid=(pl.cdiv(width, step),),
        ins=[VMEM, VMEM, rows_of(which[0]), rows_of(which[1]), across, across],
        outspecs=[out] * 3,
    )


def back_two(order, dgates, dups, w_gate, w_up, bases, piece, step=256):
    many = len(dgates)
    depth, width = w_gate.shape
    rows = many * dgates[0].shape[0]

    def body(base, *refs):
        wg, wu, out = refs[2 * many :]
        value = nt(stack(refs[:many]), wg[...]) + nt(stack(refs[many : 2 * many]), wu[...])
        put_pieces(out, value, base, piece)

    weight = pl.BlockSpec((step, width), lambda i: (i, 0))
    return order.call(
        body,
        (*dgates, *dups, w_gate, w_up),
        [spec((rows, depth))],
        smem=(bases,),
        grid=(depth // step,),
        ins=[VMEM] * (2 * many) + [weight, weight],
        outspecs=[pl.BlockSpec((rows, step), lambda i: (0, i))],
        weight=1,
    )[0]


def down_rows(order, hiddens, w_down, bases, piece, step=512):
    many = len(hiddens)
    width, depth = w_down.shape
    rows = many * hiddens[0].shape[0]

    def body(base, *refs):
        wd, out = refs[many:]
        put_pieces(out, nn(stack(refs[:many]), wd[...]), base, piece)

    return order.call(
        body,
        (*hiddens, w_down),
        [spec((rows, depth))],
        smem=(bases,),
        grid=(depth // step,),
        ins=[VMEM] * many + [pl.BlockSpec((width, step), lambda i: (0, i))],
        outspecs=[pl.BlockSpec((rows, step), lambda i: (0, i))],
    )[0]


def norm_back(h, gain, grad):
    inv = lax.rsqrt(jnp.mean(h * h, axis=1, keepdims=True) + EPS)
    scaled = grad * gain
    mean = jnp.mean(h * scaled, axis=1, keepdims=True)
    return inv * (scaled - h * (inv * inv * mean)), jnp.sum(grad * h * inv, axis=0, keepdims=True)


def second_back(order, h_one, ct, total, gain, scal, steps=2):
    rows, width = h_one.shape

    def body(s, h_ref, ct_ref, total_ref, gain_ref, dh, gsum, out):
        @pl.when(pl.program_id(0) == 0)
        def _():
            gsum[...] = jnp.zeros_like(gsum)

        grad, gain_grad = norm_back(h_ref[...], gain_ref[...], total_ref[...].astype(F32))
        value = ct_ref[...].astype(F32) * s[1] + grad
        dh[...] = value
        gsum[...] += gain_grad
        out[...] = (s[0] * value).astype(BF16)

    block = pl.BlockSpec((rows // steps, width), lambda i: (i, 0))
    row = pl.BlockSpec((1, width), lambda i: (0, 0))
    return order.call(
        body,
        (h_one, ct, total, gain),
        [spec((rows, width), F32), spec((1, width), F32), spec((rows, width))],
        smem=(scal,),
        grid=(steps,),
        ins=[block, block, block, row],
        outspecs=[block, row, block],
    )


def first_back(order, x, dh, total, gain, steps=2):
    rows, width = x.shape

    def body(x_ref, dh_ref, total_ref, gain_ref, out, gsum):
        @pl.when(pl.program_id(0) == 0)
        def _():
            gsum[...] = jnp.zeros_like(gsum)

        grad, gain_grad = norm_back(
            x_ref[...].astype(F32), gain_ref[...], total_ref[...].astype(F32)
        )
        out[...] = dh_ref[...] + grad
        gsum[...] += gain_grad

    block = pl.BlockSpec((rows // steps, width), lambda i: (i, 0))
    row = pl.BlockSpec((1, width), lambda i: (0, 0))
    return order.call(
        body,
        (x, dh, total, gain),
        [spec((rows, width), F32), spec((1, width), F32)],
        grid=(steps,),
        ins=[block, block, block, row],
        outspecs=[block, row],
    )


def mix(order, h_one, total, scal):
    def body(s, h_ref, total_ref, out):
        out[...] = (h_ref[...] + s[0] * total_ref[...].astype(F32)).astype(BF16)

    return pointwise(order, body, (h_one, total), [spec(h_one.shape)], smem=(scal,), steps=2)[0]


def back_out(order, grad_a, w_out, steps=2):
    rows, depth = grad_a.shape
    width = w_out.shape[0]

    def body(a_ref, wo, out):
        out[...] = nt(a_ref[...], wo[...]).astype(BF16)

    return order.call(
        body,
        (grad_a, w_out),
        [spec((rows, width))],
        grid=(steps,),
        ins=[pl.BlockSpec((rows // steps, depth), lambda i: (i, 0)), VMEM],
        outspecs=[pl.BlockSpec((rows // steps, width), lambda i: (i, 0))],
    )[0]


def attend_back(order, qs, k_all, v_all, grads, lses, tables, bases):
    count = len(qs)
    piece, width = qs[0].shape
    rows = 2 * piece
    heads = width // HD
    total, kv_width = k_all.shape
    groups = kv_width // HD
    share = heads // groups
    factor = 1.0 / math.sqrt(HD)

    def body(base, *refs):
        q_in, lse_in = refs[:count], refs[count : 2 * count]
        do_ref, k_ref, v_ref, cos_ref, sin_ref, out, q_ref, lse_ref, dq, dk, dv = refs[2 * count :]
        for p in range(count):
            at = pl.ds(pl.multiple_of(base[p], piece), piece)
            q_ref[at, :] = q_in[p][...]
            lse_ref[at, :] = lse_in[p][...]
        low = lax.broadcasted_iota(jnp.int32, (rows, rows), 1) <= lax.broadcasted_iota(
            jnp.int32, (rows, rows), 0
        )
        dk[...] = jnp.zeros_like(dk)
        dv[...] = jnp.zeros_like(dv)
        for i in range(total // rows):
            here = slice(i * rows, (i + 1) * rows)
            for h in range(heads):
                g = h // share
                cols = slice(h * HD, (h + 1) * HD)
                kv = slice(g * HD, (g + 1) * HD)
                query, grad = q_ref[here, cols], do_ref[here, cols]
                lse = lse_ref[here, h : h + 1]
                probs, dps = [], []
                for j in range(i + 1):
                    there = slice(j * rows, (j + 1) * rows)
                    prob = jnp.exp(nt(query, k_ref[there, kv]) * factor - lse)
                    probs.append(jnp.where(low, prob, 0.0) if j == i else prob)
                    dps.append(nt(grad, v_ref[there, kv]))
                delta = sum(
                    jnp.sum(p * d, axis=1, keepdims=True) for p, d in zip(probs, dps)
                )
                sum_q = jnp.zeros((rows, HD), F32)
                for j in range(i + 1):
                    there = slice(j * rows, (j + 1) * rows)
                    ds = (probs[j] * (dps[j] - delta)).astype(BF16)
                    sum_q += nn(ds, k_ref[there, kv])
                    dk[there, kv] += tn(ds, query)
                    dv[there, kv] += tn(probs[j].astype(BF16), grad)
                dq[here, cols] = sum_q
        for p in range(count):
            at = pl.ds(pl.multiple_of(base[p], piece), piece)
            to = slice(p * piece, (p + 1) * piece)
            cos, sin = cos_ref[at, :], sin_ref[at, :]
            for src, wide, start in ((dq, width, 0), (dk, kv_width, width)):
                for h in range(wide // HD):
                    w = src[at, h * HD : (h + 1) * HD] * factor
                    turned = w * cos - pltpu.roll(w, HD // 2, 1) * sin
                    out[to, start + h * HD : start + (h + 1) * HD] = turned.astype(BF16)
            out[to, width + kv_width :] = dv[at, :].astype(BF16)

    return order.call(
        body,
        (*qs, *lses, grads, k_all, v_all, *tables),
        [spec((total, width + 2 * kv_width))],
        smem=(bases,),
        scratch=[
            pltpu.VMEM((total, width), BF16),
            pltpu.VMEM((total, heads), F32),
            pltpu.VMEM((total, width), F32),
            pltpu.VMEM((total, kv_width), F32),
            pltpu.VMEM((total, kv_width), F32),
        ],
    )[0]


def back_one(order, grads, weights, bases, piece, step=512):
    rows, total = grads.shape
    depth = weights[0].shape[0]
    edges = [0]
    for w in weights:
        edges.append(edges[-1] + w.shape[1])

    def body(base, g_ref, *refs):
        value = sum(
            nt(g_ref[:, edges[i] : edges[i + 1]], refs[i][...]) for i in range(len(weights))
        )
        put_pieces(refs[-1], value, base, piece)

    return order.call(
        body,
        (grads, *weights),
        [spec((rows, depth))],
        smem=(bases,),
        grid=(depth // step,),
        ins=[VMEM] + [pl.BlockSpec((step, w.shape[1]), lambda i: (i, 0)) for w in weights],
        outspecs=[pl.BlockSpec((rows, step), lambda i: (0, i))],
    )[0]


class Job:
    def __init__(self, groups, outs, halves):
        self.groups, self.outs = groups, outs
        self.pairs = [pair for group in groups for pair in group]
        self.rows = self.pairs[0][0][0].shape[1]
        self.chunks, at = [], 0
        for half in halves:
            self.chunks.append((at, half))
            at += 2 * half
        self.widths = [sum(n for _, right, _ in group for _, _, n in right[:1]) for group in groups]
        self.results = [() for _ in groups]
        self.got = {}


def product(order, job, pick, chunks, bases, piece, add_to=None):
    start, half = job.chunks[chunks[0]]
    first, count, many = start // half, len(chunks), len(job.groups)
    width = job.widths[0]
    lefts, places = [], []
    for left, _, _ in job.pairs:
        if not any(left is known for known, _ in places):
            places.append((left, len(lefts)))
            lefts += left
    rights = [window for _, right, _ in job.pairs for window in right]
    total = sum(p.shape[0] for p in job.pairs[0][0])
    extra = 0 if add_to is None else 1
    got_array, got_at = add_to if extra else (None, 0)

    def body(pick_ref, base, *refs):
        left_refs, refs = refs[: len(lefts)], refs[len(lefts) :]
        right_refs, refs = refs[: len(rights)], refs[len(rights) :]
        got, outs, whole = refs[:extra], refs[extra:-1], refs[-1]

        @pl.when(pl.program_id(0) == 0)
        def _():
            at, n = 0, 0
            for _, right, placed in job.pairs:
                wide = right[0][2]
                value = stack(right_refs[n : n + len(right)])
                here = slice(at, at + wide)
                if placed:
                    put_pieces(whole, value, base, piece, here)
                else:
                    whole[:, here] = value
                at += wide
                n += len(right)

        stacks = {
            start: stack(left_refs[start : start + len(left)]) for left, start in places
        }
        at = 0
        for g, group in enumerate(job.groups):
            put = 0
            for left, right, _ in group:
                wide = right[0][2]
                start = next(s for known, s in places if known is left)
                value = tn(stacks[start], whole[:, at : at + wide])
                here = slice(put, put + wide)
                if extra:
                    mine = slice(g * half, (g + 1) * half)
                    value = (value + got[0][mine, here].astype(F32)).astype(BF16)
                    for i in range(count):

                        @pl.when(pl.program_id(0) == i)
                        def _():
                            outs[i * many + g][:, here] = value
                else:
                    outs[0][g * half : (g + 1) * half, here] = value.astype(BF16)
                at += wide
                put += wide

    block = pl.BlockSpec((many * half, width), lambda i, pick_ref, base: (i, 0))
    if extra:
        outs, outspecs = [spec((half, width))] * (count * many), None
    else:
        outs, outspecs = [spec((count * many * half, width))], [block]
    return order.call(
        body,
        (*lefts, *[array for array, _, _ in rights], *([got_array] if extra else [])),
        outs,
        prefetch=(pick, bases),
        grid=(count,),
        ins=[
            pl.BlockSpec((p.shape[0], half), lambda i, pick_ref, base: (0, first + 2 * i + pick_ref[0]))
            for p in lefts
        ]
        + [
            pl.BlockSpec((array.shape[0], n), lambda i, pick_ref, base, at=at // n: (0, at))
            for array, at, n in rights
        ]
        + [
            pl.BlockSpec((many * half, width), lambda i, pick_ref, base: (i + got_at, 0))
        ]
        * extra,
        outspecs=outspecs,
        scratch=[pltpu.VMEM((total, sum(job.widths)), BF16)],
    )


def lay(order, job, group, core, chunk, mine, other):
    start, half = job.chunks[chunk]

    def body(core_ref, mine_ref, other_ref, *outs):
        for n, ref in ((0, mine_ref), (1, other_ref)):

            @pl.when(pl.program_id(0) == n)
            def _():
                for (at, width, turned, _, _), out in zip(job.outs[group], outs):
                    value = ref[:, at : at + width].astype(F32)
                    out[...] = value.T if turned else value

    shapes, specs = [], []
    for _, width, turned, whole, place in job.outs[group]:
        if turned:
            shapes.append(pltpu.HBM((whole, job.rows), F32))
            specs.append(
                pl.BlockSpec(
                    (width, half),
                    lambda n, core_ref, p=place: (p, start // half + (core_ref[0] ^ n)),
                )
            )
        else:
            shapes.append(pltpu.HBM((job.rows, whole), F32))
            specs.append(
                pl.BlockSpec(
                    (half, width),
                    lambda n, core_ref, p=place: (start // half + (core_ref[0] ^ n), p),
                )
            )
    job.results[group] = order.call(
        body,
        (mine, other),
        shapes,
        prefetch=(core,),
        grid=(2,),
        outspecs=specs,
        reuse=job.results[group],
    )


class Line:
    LAG = 2

    def __init__(self, order, size, bases, piece):
        self.order, self.size, self.bases, self.piece = order, size, bases, piece
        where = lax.axis_index("dp")
        core, z = where % 2, where // 2
        self.mine = core.reshape(1).astype(jnp.int32)
        self.other = (1 - core).reshape(1).astype(jnp.int32)
        self.middle = ((z == 1) | (z == 2)).astype(jnp.int32).reshape(1)
        self.count = 0
        self.chunks = []
        self.part, self.fold, self.half, self.mids = [], {}, {}, {}
        self.whole, self.ends, self.final, self.done = {}, {}, {}, {}

    def hop(self, value, steps):
        pairs = [(2 * a + c, 2 * b + c) for a, b in steps for c in range(2)]
        return lax.ppermute(value, "dp", pairs)

    def send(self, job, chunks):
        part = product(self.order, job, self.other, chunks, self.bases, self.piece)[0]
        got = swap(part, "dp", self.size, 1)
        for n, k in enumerate(chunks):
            job.got[k] = (got, n)

    def enter(self, job, chunks):
        got = job.got[chunks[0]]
        parts = iter(product(self.order, job, self.mine, chunks, self.bases, self.piece, got))
        for k in chunks:
            for group in range(len(job.groups)):
                part = next(parts)
                n = len(self.part)
                if n < 2 * self.LAG:
                    self.fold[n] = self.hop(part, [(0, 1), (3, 2)])
                self.chunks.append((job, group, k))
                self.part.append(part)

    def tick(self, k):
        b, c, ahead = k - self.LAG, k - 2 * self.LAG, k + self.LAG
        here, back, out = k < self.count, 0 <= b < self.count, 0 <= c < self.count
        on = 2 * self.LAG <= ahead < self.count
        merged = back and on and self.half[b].shape == self.part[ahead].shape
        operands, outs = [], []
        if here:
            operands += [self.part[k], self.fold[k]]
            outs.append(spec(self.part[k].shape))
        if back:
            operands += [self.half[b], self.mids[b]]
            outs.append(spec(self.half[b].shape))
        if merged:
            operands.append(self.part[ahead])
        if out:
            operands += [self.whole[c], self.ends[c]]
            outs.append(spec(self.whole[c].shape))

        def body(flag, *refs):
            middle = flag[0] != 0
            refs, results = list(refs[: len(operands)]), list(refs[len(operands) :])
            if here:
                results.pop(0)[...] = plus(refs.pop(0), refs.pop(0)).astype(BF16)
            if back:
                both = plus(refs.pop(0), refs.pop(0)).astype(BF16)
                results.pop(0)[...] = jnp.where(middle, both, refs.pop(0)[...]) if merged else both
            if out:
                results.pop(0)[...] = jnp.where(middle, refs.pop(0)[...], refs.pop(0)[...])

        wait = [self.done[c - 1]] if c - 1 in self.done else []
        got = list(pointwise(self.order, body, operands, outs, smem=(self.middle,), wait=wait))
        if here:
            self.half[k] = got.pop(0)
        if back:
            self.whole[b] = got.pop(0)
        if out:
            self.final[c] = got.pop(0)
        if here:
            self.mids[k] = self.hop(self.half[k], [(1, 2), (2, 1)])
        if merged:
            both = self.hop(self.whole[b], [(0, 1), (1, 0), (2, 3), (3, 2)])
            self.ends[b] = self.fold[ahead] = both
        else:
            if back:
                self.ends[b] = self.hop(self.whole[b], [(1, 0), (2, 3)])
            if on:
                self.fold[ahead] = self.hop(self.part[ahead], [(0, 1), (3, 2)])
        if out:
            self.done[c] = swap(self.final[c], "dp", self.size, 1)

    def lay(self, i):
        if 0 <= i < self.count:
            job, group, k = self.chunks[i]
            lay(self.order, job, group, self.mine, k, self.final[i], self.done[i])


class SmallSum:
    def __init__(self, order, value, mesh_shape):
        self.order, self.value = order, value
        self.steps = []
        for axis in ("tensor", "dp"):
            size, bit = mesh_shape[axis], 1
            if size & (size - 1):
                self.steps.append((axis, size, None))
                continue
            while bit < size:
                self.steps.append((axis, size, bit))
                bit *= 2

    def step(self):
        if self.steps:
            axis, size, bit = self.steps.pop(0)
            if bit is None:
                self.value = lax.psum(self.value, axis)
            else:
                self.value = add(self.order, self.value, swap(self.value, axis, size, bit))


def local(
    mesh_shape,
    tokens,
    cotangent,
    w_query,
    w_key,
    w_value,
    w_output,
    w_gate,
    w_up,
    w_down,
    gain_attn,
    gain_mlp,
    dropped,
    exit_scale,
    positions,
):
    x, ct = tokens[0], cotangent[0]
    order = Order()
    square = mesh_shape["tensor"] == 4 and mesh_shape["dp"] == 8
    rows = Rows(mesh_shape["tensor"], x.shape[0], square)
    bases = rows.bases
    line = Line(order, mesh_shape["dp"], bases, rows.piece)
    pieces = 2 if square else 1
    scal = jnp.stack([1.0 - dropped[0].astype(F32), exit_scale[0]])
    gain_one, gain_two = gain_attn[None], gain_mlp[None]
    attn_weights = (w_query, w_key, w_value)

    freqs = jnp.exp(jnp.arange(HD // 2, dtype=F32) * (-2.0 * math.log(10000.0) / HD))
    turned = positions[0].astype(F32)[:, None] * freqs[None, :]
    cos, sin = jnp.cos(turned), jnp.sin(turned)
    tables = (jnp.concatenate([cos, cos], axis=1), jnp.concatenate([-sin, sin], axis=1))

    n_own, grad_m_own = prepare(order, x, ct, gain_one, scal, pieces)
    qs, ks, vs = {}, {}, {}

    def project_group(group, n_one):
        last = group is rows.groups[-1]
        done = [(ks[i], vs[i]) for i in sorted(ks)] if last else None
        got = project(
            order, [n_one[i] for i in group], attn_weights, tables, bases, group, done
        )
        for n, i in enumerate(group):
            qs[i], ks[i], vs[i] = got[n], got[2 + n], got[4 + n]
        return got[6:]

    if square:
        n_one = rows.gather_first(n_own)
        project_group(rows.groups[0], n_one)
        n_one += rows.gather_second(order.tie(*n_own))
        n_one += rows.gather_third(*order.tie(n_one[2], n_one[3]))
        project_group(rows.groups[1], n_one)
        project_group(rows.groups[2], n_one)
        grad_m = rows.gather_all(order.tie(grad_m_own))
        k_all, v_all = project_group(rows.groups[3], n_one)
    else:
        n_one = rows.gather_whole(n_own[0])
        grad_m = rows.gather_all(grad_m_own)
        for group in rows.groups:
            k_all, v_all = project_group(group, n_one) or (None, None)

    attn, lses, parts = {}, {}, {}

    def attend_block(block):
        got = attend(order, [qs[i] for i in block], k_all, v_all, w_output, bases, block[0])
        for n, i in enumerate(block):
            attn[i], lses[i], parts[i] = got[n], got[2 + n], got[4 + n]

    out_sum = Scatter(order, rows)
    if square:
        attend_block(rows.blocks[0])
        out_sum.far({i: parts[i] for i in (6, 7)})
        attend_block(rows.blocks[1])
        attend_block(rows.blocks[2])
        out_sum.near({i: parts[i] for i in (2, 3)})
        out_sum.rest({i: parts[i] for i in (4, 5)})
        attend_block(rows.blocks[3])
        out_sum.own({i: parts[i] for i in (0, 1)})
    else:
        for block in rows.blocks:
            attend_block(block)
        out_sum.own(parts)
    h_one, n_two_own = second_norm(order, x, out_sum.result(), gain_two, scal, pieces)

    hidden, dgate, dup = [], [], []
    dhid = back_hidden(order, grad_m, w_down)

    def feed(g):
        group = rows.groups[g]
        got = feed_forward(
            order, [n_two[i] for i in group], dhid, w_gate, w_up, bases, group
        )
        for made, values in zip(got, (hidden, dgate, dup)):
            values.append(made)

    every = range(rows.count)
    if square:
        n_two = rows.gather_first(n_two_own)
        n_two += rows.gather_second(n_two_own)
        feed(0)
        n_two += rows.gather_third(*order.tie(n_two[2], n_two[3]))
        feed(1)
        feed(2)
        feed(3)
    else:
        n_two = rows.gather_whole(n_two_own[0])
        for g in range(len(rows.groups)):
            feed(g)

    def back_two_all():
        return rows.scatter_all(
            back_two(order, dgate, dup, w_gate, w_up, bases, rows.piece)
        )

    def second_back_all(total):
        return second_back(order, h_one, ct, total, gain_two, scal)

    def attend_back_all(grad_a):
        return attend_back(
            order,
            [qs[i] for i in every],
            k_all,
            v_all,
            back_out(order, grad_a, w_output),
            [lses[i] for i in every],
            tables,
            bases,
        )

    def back_one_all(gqkv):
        return rows.scatter_all(back_one(order, gqkv, attn_weights, bases, rows.piece))

    def down_all():
        return rows.scatter_all(down_rows(order, hidden, w_down, bases, rows.piece))

    ff, width, kv = w_gate.shape[1], w_query.shape[1], w_key.shape[1]
    def whole_of(arrays):
        return [(array, 0, array.shape[1]) for array in arrays]

    ff_out = [[(0, ff, False, ff, 0)]]
    down = Job([[([grad_m], whole_of(hidden), True)]], [[(0, ff, True, ff, 0)]], [256] * 4)
    wide = Job(
        [[(n_two, whole_of(dgate), False)], [(n_two, whole_of(dup), False)]],
        ff_out * 2,
        [256] * 4,
    )

    def late_jobs(grad_a, gqkv):
        total = gqkv.shape[1]
        rest = HD if square else 0
        right = [(gqkv, 0, total - rest)]
        outs = [
            (0, width, True, width, 0),
            (width, width, False, width, 0),
            (2 * width, kv, False, kv, 0),
            (2 * width + kv, kv - rest, False, kv, 0),
        ]
        pairs = [([grad_a], whole_of([attn[i] for i in every]), True), (n_one, right, False)]
        jobs = [Job([pairs], [outs], [256, 256, 256, 128, 128])]
        if rest:
            pairs = [(n_one, [(gqkv, total - rest, rest)], False)]
            jobs.append(Job([pairs], [[(0, rest, False, kv, kv // rest - 1)]], [1024]))
        return jobs

    if square:
        line.count = 18
        line.send(down, [0, 1])
        line.send(down, [2, 3])
        line.enter(down, [0])
        two_total = back_two_all()
        line.enter(down, [1])
        line.send(wide, [0, 1])
        line.tick(0)
        line.enter(down, [2, 3])
        line.tick(1)
        line.enter(wide, [0, 1])
        line.tick(2)
        line.send(wide, [2, 3])
        line.tick(3)
        dh, gain_two_sum, grad_a_own = second_back_all(two_total)
        grad_a = rows.gather_all(grad_a_own)
        line.tick(4)
        line.enter(wide, [2, 3])
        line.tick(5)
        mix_total = down_all()
        line.tick(6)
        line.lay(0)
        line.tick(7)
        gqkv = attend_back_all(grad_a)
        late, late_rest = late_jobs(grad_a, gqkv)
        line.tick(8)
        line.send(late, [0, 1, 2])
        one_total = back_one_all(gqkv)
        line.tick(9)
        line.enter(late, [0, 1, 2])
        line.tick(10)
        line.send(late, [3, 4])
        line.send(late_rest, [0])
        line.tick(11)
        line.lay(1)
        line.enter(late, [3, 4])
        line.enter(late_rest, [0])
        line.tick(12)
        line.lay(2)
        line.lay(3)
        line.tick(13)
        line.lay(4)
        line.lay(5)
        laid = 6
        for k in range(14, line.count + 2 * line.LAG):
            line.tick(k)
            if k == 14:
                mixed = mix(order, h_one, mix_total, scal)
                input_grad, gain_one_sum = first_back(order, x, dh, one_total, gain_one)
                gains = SmallSum(
                    order, jnp.concatenate([gain_one_sum, gain_two_sum]), mesh_shape
                )
            while laid <= min(k - 5, laid + 2) and laid < 6 + 2 * (k - 13):
                line.lay(laid)
                laid += 1
            if k in (15, 16, 17, 18, 20):
                gains.step()
        while laid < line.count - 1:
            line.lay(laid)
            laid += 1
        late_rest.results[0] = (late.results[0][3],)
        line.lay(line.count - 1)
        gain_sums = gains.value
    else:
        dh, gain_two_sum, grad_a_own = second_back_all(back_two_all())
        grad_a = rows.gather_all(grad_a_own)
        gqkv = attend_back_all(grad_a)
        (late,) = late_jobs(grad_a, gqkv)
        mixed = mix(order, h_one, down_all(), scal)
        input_grad, gain_one_sum = first_back(order, x, dh, back_one_all(gqkv), gain_one)
        gains = SmallSum(order, jnp.concatenate([gain_one_sum, gain_two_sum]), mesh_shape)
        while gains.steps:
            gains.step()
        gain_sums = gains.value
        for job in (down, wide, late):
            for n, group in enumerate(job.groups):
                parts = [
                    tn(jnp.concatenate(a), jnp.concatenate([array for array, _, _ in b]))
                    for a, b, _ in group
                ]
                whole = jnp.concatenate(parts, axis=1).astype(BF16)
                whole = lax.psum(whole, "dp").astype(F32)
                job.results[n] = [
                    whole[:, at : at + size].T if turned else whole[:, at : at + size]
                    for at, size, turned, _, _ in job.outs[n]
                ]
    grad_output, grad_query, grad_key, grad_value = late.results[0]
    if square:
        grad_value = late_rest.results[0][0]
    return (
        mixed[None],
        input_grad[None],
        grad_query,
        grad_key,
        grad_value,
        grad_output,
        wide.results[0][0],
        wide.results[1][0],
        down.results[0][0],
        gain_sums[0],
        gain_sums[1],
    )


def solution(mesh):
    shape = dict(mesh.shape)
    placed = (
        P("dp", "tensor", None),
        P("dp", "tensor", None),
        P(None, "tensor"),
        P(None, "tensor"),
        P(None, "tensor"),
        P("tensor", None),
        P(None, "tensor"),
        P(None, "tensor"),
        P("tensor", None),
        P(),
        P(),
        P("dp"),
        P("dp"),
        P("dp", None),
    )

    def step(*args):
        return local(shape, *args)

    return jax.shard_map(
        step,
        mesh=mesh,
        in_specs=placed,
        out_specs=(
            P("dp", "tensor", None),
            P("dp", "tensor", None),
            P(None, "tensor"),
            P(None, "tensor"),
            P(None, "tensor"),
            P("tensor", None),
            P(None, "tensor"),
            P(None, "tensor"),
            P("tensor", None),
            P(),
            P(),
        ),
        check_vma=False,
    )
```

```python
import functools
import math

import jax
import jax.numpy as jnp
from jax import lax
from jax.experimental import pallas as pl
from jax.experimental.pallas import tpu as pltpu
from jax.sharding import PartitionSpec as P

HD = 128
EPS = 1e-05
F32 = jnp.float32
BF16 = jnp.bfloat16
VMEM = pl.BlockSpec(memory_space=pltpu.VMEM)
SMEM = pl.BlockSpec(memory_space=pltpu.SMEM)
HBM = pl.BlockSpec(memory_space=pltpu.HBM)
STEP_FLOPS, STEP_BYTES = 20_000_000_000, 120_000_000
MIB = 1024 * 1024
LIMIT = 28


def spec(shape, dtype=BF16):
    return jax.ShapeDtypeStruct(tuple(shape), dtype)


def mm(a, b, dims):
    return lax.dot_general(a, b, (dims, ((), ())), preferred_element_type=F32)


def nn(a, b):
    return mm(a, b, ((1,), (0,)))


def nt(a, b):
    return mm(a, b, ((1,), (1,)))


def tn(a, b):
    return mm(a, b, ((0,), (0,)))


def stack(refs):
    return jnp.concatenate([r[...] for r in refs], axis=0)


def tiles(total, step):
    return [(at, min(step, total - at)) for at in range(0, total, step)]


def put_rows(refs, value, cols=slice(None)):
    rows = refs[0].shape[0]
    for i, ref in enumerate(refs):
        ref[:, cols] = value[i * rows : (i + 1) * rows].astype(ref.dtype)


def in_hbm(value):
    return pltpu.with_memory_space_constraint(value, pltpu.HBM)


class Order:
    def __init__(self):
        self.last = ()

    def tie(self, *values):
        if not self.last:
            return values if len(values) > 1 else values[0]
        out = lax.optimization_barrier((self.last[0], *values))[1:]
        return out if len(values) > 1 else out[0]

    def call(
        self,
        body,
        operands,
        outs,
        smem=(),
        prefetch=(),
        scratch=(),
        grid=(),
        ins=None,
        outspecs=None,
        reuse=(),
        wait=(),
        weight=1,
    ):
        ahead, total = len(prefetch) + len(smem), len(prefetch) + len(smem) + len(operands)
        last = (*self.last, *wait)
        skip = len(last) + len(reuse)

        def kernel(*refs):
            results = refs[total + skip :]
            body(*refs[:total], *results[: len(outs)], *results[len(outs) + 1 :])

        got = pl.pallas_call(
            kernel,
            out_shape=(*outs, pltpu.HBM((8, 128), F32)),
            grid_spec=pltpu.PrefetchScalarGridSpec(
                num_scalar_prefetch=len(prefetch),
                grid=grid,
                in_specs=[SMEM] * len(smem)
                + list(ins or [VMEM] * len(operands))
                + [HBM] * skip,
                out_specs=(*(outspecs or [VMEM] * len(outs)), HBM),
                scratch_shapes=scratch,
            ),
            input_output_aliases={total + len(last) + n: n for n in range(len(reuse))},
            cost_estimate=pl.CostEstimate(
                flops=weight * STEP_FLOPS, bytes_accessed=weight * STEP_BYTES, transcendentals=0
            ),
            compiler_params=pltpu.CompilerParams(vmem_limit_bytes=LIMIT * MIB),
        )(*prefetch, *smem, *operands, *map(in_hbm, (*last, *reuse)))
        self.last = (got[-1],)
        return got[:-1]


def swap(value, axis, size, bit):
    return lax.ppermute(value, axis, [(i, i ^ bit) for i in range(size)])


def row_blocks(arrays, steps):
    return [pl.BlockSpec((a.shape[0] // steps, a.shape[1]), lambda i: (i, 0)) for a in arrays]


def pointwise(order, body, operands, outs, smem=(), steps=1, wait=()):
    return order.call(
        body,
        operands,
        outs,
        smem=smem,
        grid=(steps,),
        ins=row_blocks(operands, steps),
        outspecs=row_blocks(outs, steps),
        wait=wait,
    )


def plus(a_ref, b_ref):
    return a_ref[...].astype(F32) + b_ref[...].astype(F32)


def add(order, a, b):
    def body(a_ref, b_ref, out):
        out[...] = plus(a_ref, b_ref).astype(out.dtype)

    return pointwise(order, body, (a, b), [spec(a.shape, a.dtype)])[0]


class Rows:
    def __init__(self, size, own_rows, square):
        self.size = size
        self.square = square
        me = lax.axis_index("tensor")
        if self.square:
            half = own_rows // 2
            where = [(0, 0), (0, 1), (1, 0), (2, 1), (1, 1), (2, 0), (3, 0), (3, 1)]
            self.bases = jnp.stack([(me ^ r) * own_rows + h * half for r, h in where])
            self.piece = half
            self.blocks = [(6, 7), (2, 4), (5, 3), (0, 1)]
        else:
            self.bases = jnp.arange(size, dtype=jnp.int32) * own_rows
            self.piece = own_rows
            self.blocks = [(i, i + 1) for i in range(0, size, 2)]
        self.count = self.bases.shape[0]
        self.groups = [(i, i + 1) for i in range(0, self.count, 2)]
        self.own = [0, 1] if self.square else None

    def swap(self, value, bit):
        return swap(value, "tensor", self.size, bit)

    def gather_first(self, pieces):
        top, low = pieces
        return [top, low, self.swap(top, 1), self.swap(low, 2)]

    def gather_second(self, pieces):
        top, low = pieces
        return [self.swap(low, 1), self.swap(top, 2)]

    def gather_third(self, x_top, y_low):
        return [self.swap(x_top, 2), self.swap(y_low, 1)]

    def gather_all(self, block):
        return lax.all_gather(block, "tensor", axis=0, tiled=True)

    def gather_whole(self, block):
        return jnp.split(self.gather_all(block), self.size, axis=0)

    def scatter_all(self, whole):
        return lax.psum_scatter(whole, "tensor", scatter_dimension=0, tiled=True)

    def scatter_whole(self, pieces):
        return [[self.scatter_all(jnp.concatenate(pieces, axis=0))]]


class Scatter:
    def __init__(self, order, rows):
        self.order, self.rows, self.parts = order, rows, {}

    def far(self, pieces):
        self.parts.update(pieces)
        if self.rows.square:
            self.y_top = self.rows.swap(pieces[6], 1)
            self.x_low = self.rows.swap(pieces[7], 2)

    def near(self, pieces):
        self.parts.update(pieces)
        if self.rows.square:
            self.x_got_top = self.rows.swap(pieces[2], 1)
            self.y_got_low = self.rows.swap(pieces[3], 2)

    def rest(self, pieces):
        self.parts.update(pieces)
        if self.rows.square:
            self.x_got_low = self.rows.swap(add(self.order, pieces[4], self.x_low), 1)
            self.y_got_top = self.rows.swap(add(self.order, pieces[5], self.y_top), 2)

    def own(self, pieces):
        self.parts.update(pieces)

    def result(self):
        if not self.rows.square:
            return self.rows.scatter_whole([self.parts[i] for i in range(self.rows.count)])
        return [
            [self.parts[0], self.parts[1]],
            [self.x_got_top, self.x_got_low],
            [self.y_got_top, self.y_got_low],
        ]


class Pieced:
    def __init__(self, pieces, rows, width, steps=1):
        self.pieces, self.steps, self.width = pieces, steps, width
        self.grid = (pieces, steps)
        self.block = rows // (pieces * steps)
        self.whole = pl.BlockSpec((self.block, width), lambda p, i: (p * steps + i, 0))
        self.row = pl.BlockSpec((1, width), lambda p, i: (0, 0))

    def piece(self, q):
        last = self.steps - 1
        return pl.BlockSpec(
            (self.block, self.width),
            lambda p, i: (jnp.where(p == q, i, jnp.where(p < q, 0, last)), 0),
        )

    def lists(self, count):
        return [self.piece(q) for _ in range(count) for q in range(self.pieces)]

    def each(self, step):
        for q in range(self.pieces):
            pl.when(pl.program_id(0) == q)(lambda q=q: step(q))

    def total(self, refs, q):
        return sum(ref[...].astype(F32) for ref in refs[q :: self.pieces])


def prepare(order, x, ct, gain, scal, pieces):
    rows, width = x.shape
    plan = Pieced(pieces, rows, width)

    def body(s, x_ref, ct_ref, gain_ref, grad, *outs):
        def step(q):
            value = x_ref[...].astype(F32)
            inv = lax.rsqrt(jnp.mean(value * value, axis=1, keepdims=True) + EPS)
            outs[q][...] = (value * inv * gain_ref[...]).astype(BF16)
            grad[...] = (s[0] * (ct_ref[...].astype(F32) * s[1])).astype(BF16)

        plan.each(step)

    grad, *outs = order.call(
        body,
        (x, ct, gain),
        [spec((rows, width))] + [spec((rows // pieces, width))] * pieces,
        smem=(scal,),
        grid=plan.grid,
        ins=[plan.whole, plan.whole, plan.row],
        outspecs=[plan.whole, *plan.lists(1)],
    )
    return outs, grad


def project(order, pieces, weights, tables, bases, which, earlier=None):
    rows = pieces[0].shape[0]
    width, kv = weights[0].shape[1], weights[1].shape[1]
    many = 0 if earlier is None else len(earlier)
    total = tables[0].shape[0]

    def body(base, a_ref, b_ref, wq, wk, wv, cos_ref, sin_ref, *refs):
        olds, outs = refs[: 2 * many], refs[2 * many :]
        block = stack([a_ref, b_ref])
        ats = [pl.ds(pl.multiple_of(base[i], rows), rows) for i in which]
        cos = jnp.concatenate([cos_ref[at, :] for at in ats])
        sin = jnp.concatenate([sin_ref[at, :] for at in ats])

        def turn(value, refs_out):
            for h in range(value.shape[1] // HD):
                cols = slice(h * HD, (h + 1) * HD)
                u = value[:, cols]
                put_rows(refs_out, u * cos + pltpu.roll(u, HD // 2, 1) * sin, cols)

        turn(nn(block, wq[...]), outs[0:2])
        turn(nn(block, wk[...]), outs[2:4])
        put_rows(outs[4:6], nn(block, wv[...]))
        if many:
            k_all, v_all = outs[6:8]
            done = [i for i in range(many + 2) if i not in which]
            for n, i in enumerate(done):
                at = pl.ds(pl.multiple_of(base[i], rows), rows)
                k_all[at, :] = olds[n][...]
                v_all[at, :] = olds[many + n][...]
            for n in range(2):
                k_all[ats[n], :] = outs[2 + n][...]
                v_all[ats[n], :] = outs[4 + n][...]

    outs = [spec((rows, width))] * 2 + [spec((rows, kv))] * 4
    operands = [*pieces, *weights, *tables]
    if many:
        outs += [spec((total, kv))] * 2
        operands += [k for k, _ in earlier] + [v for _, v in earlier]
    return order.call(body, operands, outs, smem=(bases,))


def attend(order, queries, k_all, v_all, w_out, bases, first):
    piece, width = queries[0].shape
    rows = 2 * piece
    heads = width // HD
    share = heads // (k_all.shape[1] // HD)
    factor = 1.0 / math.sqrt(HD)
    wide = w_out.shape[1]
    blocks = k_all.shape[0] // rows

    def body(base, qa, qb, k_ref, v_ref, wo, *outs):
        attn, lses, parts = outs[0:2], outs[2:4], outs[4:6]
        query_all = stack([qa, qb])
        low = lax.broadcasted_iota(jnp.int32, (rows, rows), 1) <= lax.broadcasted_iota(
            jnp.int32, (rows, rows), 0
        )
        place = base[first] // rows

        def upto(n):
            for h in range(heads):
                g = h // share
                cols = slice(h * HD, (h + 1) * HD)
                kv = slice(g * HD, (g + 1) * HD)
                query = query_all[:, cols]
                raw = [nt(query, k_ref[j * rows : (j + 1) * rows, kv]) for j in range(n)]
                raw[-1] = jnp.where(low, raw[-1], -1e30)
                top = functools.reduce(
                    jnp.maximum, [jnp.max(s, axis=1, keepdims=True) for s in raw]
                )
                powers = [jnp.exp((s - top) * factor) for s in raw]
                total = sum(jnp.sum(p, axis=1, keepdims=True) for p in powers)
                mixed = sum(
                    nn(powers[j].astype(BF16), v_ref[j * rows : (j + 1) * rows, kv])
                    for j in range(n)
                )
                put_rows(attn, mixed / total, cols)
                put_rows(lses, top * factor + jnp.log(total), slice(h, h + 1))

        for n in range(1, blocks + 1):
            pl.when(place == n - 1)(functools.partial(upto, n))
        value = stack(attn)
        for at, size in tiles(wide, 512):
            put_rows(parts, nn(value, wo[:, at : at + size]), slice(at, at + size))

    return order.call(
        body,
        (*queries, k_all, v_all, w_out),
        [spec((piece, width))] * 2 + [spec((piece, heads), F32)] * 2 + [spec((piece, wide))] * 2,
        smem=(bases,),
    )


def second_norm(order, x, sums, gain, scal, pieces):
    rows, width = x.shape
    plan = Pieced(pieces, rows, width)
    count = len(sums)

    def body(s, x_ref, gain_ref, *refs):
        h_one, *outs = refs[count * pieces :]

        def step(q):
            value = x_ref[...].astype(F32) + s[0] * plan.total(refs[: count * pieces], q)
            h_one[...] = value
            inv = lax.rsqrt(jnp.mean(value * value, axis=1, keepdims=True) + EPS)
            outs[q][...] = (value * inv * gain_ref[...]).astype(BF16)

        plan.each(step)

    got = order.call(
        body,
        (x, gain, *[p for s in sums for p in s]),
        [spec((rows, width), F32)] + [spec((rows // pieces, width))] * pieces,
        smem=(scal,),
        grid=plan.grid,
        ins=[plan.whole, plan.row, *plan.lists(count)],
        outspecs=[plan.whole, *plan.lists(1)],
    )
    return got[0], list(got[1:])


def put_pieces(out, value, base, piece, cols=slice(None)):
    for p in range(value.shape[0] // piece):
        at = pl.ds(pl.multiple_of(base[p], piece), piece)
        out[at, cols] = value[p * piece : (p + 1) * piece].astype(out.dtype)


def back_hidden(order, grad_m, w_down, step=512):
    rows, depth = grad_m.shape
    width = w_down.shape[0]

    def body(grad_ref, wd, out):
        out[...] = nt(grad_ref[...], wd[...]).astype(BF16)

    return order.call(
        body,
        (grad_m, w_down),
        [spec((rows, width))],
        grid=(pl.cdiv(width, step),),
        ins=[VMEM, pl.BlockSpec((step, depth), lambda i: (i, 0))],
        outspecs=[pl.BlockSpec((rows, step), lambda i: (0, i))],
    )[0]


def feed_forward(order, n_pieces, dhid, w_gate, w_up, bases, which, step=512):
    piece, depth = n_pieces[0].shape
    width = w_gate.shape[1]
    rows = 2 * piece

    def body(base, na, nb, da, db, wg, wu, hid, dg, du):
        n_two = stack([na, nb])
        gate = nn(n_two, wg[...])
        up = nn(n_two, wu[...])
        grad = stack([da, db]).astype(F32)
        sig = 1.0 / (1.0 + jnp.exp(-gate))
        silu = gate * sig
        hid[...] = (silu * up).astype(BF16)
        dg[...] = (grad * up * (sig + silu * (1.0 - sig))).astype(BF16)
        du[...] = (grad * silu).astype(BF16)

    def rows_of(p):
        return pl.BlockSpec((piece, step), lambda i, base: (base[p] // piece, i))

    across = pl.BlockSpec((depth, step), lambda i, base: (0, i))
    out = pl.BlockSpec((rows, step), lambda i, base: (0, i))
    return order.call(
        body,
        (*n_pieces, dhid, dhid, w_gate, w_up),
        [spec((rows, width))] * 3,
        prefetch=(bases,),
        grid=(pl.cdiv(width, step),),
        ins=[VMEM, VMEM, rows_of(which[0]), rows_of(which[1]), across, across],
        outspecs=[out] * 3,
    )


def back_two(order, dgates, dups, w_gate, w_up, bases, piece, step=256):
    many = len(dgates)
    depth, width = w_gate.shape
    rows = many * dgates[0].shape[0]

    def body(base, *refs):
        wg, wu, out = refs[2 * many :]
        value = nt(stack(refs[:many]), wg[...]) + nt(stack(refs[many : 2 * many]), wu[...])
        put_pieces(out, value, base, piece)

    weight = pl.BlockSpec((step, width), lambda i: (i, 0))
    return order.call(
        body,
        (*dgates, *dups, w_gate, w_up),
        [spec((rows, depth))],
        smem=(bases,),
        grid=(depth // step,),
        ins=[VMEM] * (2 * many) + [weight, weight],
        outspecs=[pl.BlockSpec((rows, step), lambda i: (0, i))],
        weight=1,
    )[0]


def down_rows(order, hiddens, w_down, bases, piece, step=512):
    many = len(hiddens)
    width, depth = w_down.shape
    rows = many * hiddens[0].shape[0]

    def body(base, *refs):
        wd, out = refs[many:]
        put_pieces(out, nn(stack(refs[:many]), wd[...]), base, piece)

    return order.call(
        body,
        (*hiddens, w_down),
        [spec((rows, depth))],
        smem=(bases,),
        grid=(depth // step,),
        ins=[VMEM] * many + [pl.BlockSpec((width, step), lambda i: (0, i))],
        outspecs=[pl.BlockSpec((rows, step), lambda i: (0, i))],
    )[0]


def norm_back(h, gain, grad):
    inv = lax.rsqrt(jnp.mean(h * h, axis=1, keepdims=True) + EPS)
    scaled = grad * gain
    mean = jnp.mean(h * scaled, axis=1, keepdims=True)
    return inv * (scaled - h * (inv * inv * mean)), jnp.sum(grad * h * inv, axis=0, keepdims=True)


def second_back(order, h_one, ct, total, gain, scal, steps=2):
    rows, width = h_one.shape

    def body(s, h_ref, ct_ref, total_ref, gain_ref, dh, gsum, out):
        @pl.when(pl.program_id(0) == 0)
        def _():
            gsum[...] = jnp.zeros_like(gsum)

        grad, gain_grad = norm_back(h_ref[...], gain_ref[...], total_ref[...].astype(F32))
        value = ct_ref[...].astype(F32) * s[1] + grad
        dh[...] = value
        gsum[...] += gain_grad
        out[...] = (s[0] * value).astype(BF16)

    block = pl.BlockSpec((rows // steps, width), lambda i: (i, 0))
    row = pl.BlockSpec((1, width), lambda i: (0, 0))
    return order.call(
        body,
        (h_one, ct, total, gain),
        [spec((rows, width), F32), spec((1, width), F32), spec((rows, width))],
        smem=(scal,),
        grid=(steps,),
        ins=[block, block, block, row],
        outspecs=[block, row, block],
    )


def first_back(order, x, dh, total, gain, steps=2):
    rows, width = x.shape

    def body(x_ref, dh_ref, total_ref, gain_ref, out, gsum):
        @pl.when(pl.program_id(0) == 0)
        def _():
            gsum[...] = jnp.zeros_like(gsum)

        grad, gain_grad = norm_back(
            x_ref[...].astype(F32), gain_ref[...], total_ref[...].astype(F32)
        )
        out[...] = dh_ref[...] + grad
        gsum[...] += gain_grad

    block = pl.BlockSpec((rows // steps, width), lambda i: (i, 0))
    row = pl.BlockSpec((1, width), lambda i: (0, 0))
    return order.call(
        body,
        (x, dh, total, gain),
        [spec((rows, width), F32), spec((1, width), F32)],
        grid=(steps,),
        ins=[block, block, block, row],
        outspecs=[block, row],
    )


def mix(order, h_one, total, scal):
    def body(s, h_ref, total_ref, out):
        out[...] = (h_ref[...] + s[0] * total_ref[...].astype(F32)).astype(BF16)

    return pointwise(order, body, (h_one, total), [spec(h_one.shape)], smem=(scal,), steps=2)[0]


def back_out(order, grad_a, w_out, steps=2):
    rows, depth = grad_a.shape
    width = w_out.shape[0]

    def body(a_ref, wo, out):
        out[...] = nt(a_ref[...], wo[...]).astype(BF16)

    return order.call(
        body,
        (grad_a, w_out),
        [spec((rows, width))],
        grid=(steps,),
        ins=[pl.BlockSpec((rows // steps, depth), lambda i: (i, 0)), VMEM],
        outspecs=[pl.BlockSpec((rows // steps, width), lambda i: (i, 0))],
    )[0]


def attend_back(order, qs, k_all, v_all, grads, lses, tables, bases):
    count = len(qs)
    piece, width = qs[0].shape
    rows = 2 * piece
    heads = width // HD
    total, kv_width = k_all.shape
    groups = kv_width // HD
    share = heads // groups
    factor = 1.0 / math.sqrt(HD)

    def body(base, *refs):
        q_in, lse_in = refs[:count], refs[count : 2 * count]
        do_ref, k_ref, v_ref, cos_ref, sin_ref, out, q_ref, lse_ref, dq, dk, dv = refs[2 * count :]
        for p in range(count):
            at = pl.ds(pl.multiple_of(base[p], piece), piece)
            q_ref[at, :] = q_in[p][...]
            lse_ref[at, :] = lse_in[p][...]
        low = lax.broadcasted_iota(jnp.int32, (rows, rows), 1) <= lax.broadcasted_iota(
            jnp.int32, (rows, rows), 0
        )
        dk[...] = jnp.zeros_like(dk)
        dv[...] = jnp.zeros_like(dv)
        for i in range(total // rows):
            here = slice(i * rows, (i + 1) * rows)
            for h in range(heads):
                g = h // share
                cols = slice(h * HD, (h + 1) * HD)
                kv = slice(g * HD, (g + 1) * HD)
                query, grad = q_ref[here, cols], do_ref[here, cols]
                lse = lse_ref[here, h : h + 1]
                probs, dps = [], []
                for j in range(i + 1):
                    there = slice(j * rows, (j + 1) * rows)
                    prob = jnp.exp(nt(query, k_ref[there, kv]) * factor - lse)
                    probs.append(jnp.where(low, prob, 0.0) if j == i else prob)
                    dps.append(nt(grad, v_ref[there, kv]))
                delta = sum(
                    jnp.sum(p * d, axis=1, keepdims=True) for p, d in zip(probs, dps)
                )
                sum_q = jnp.zeros((rows, HD), F32)
                for j in range(i + 1):
                    there = slice(j * rows, (j + 1) * rows)
                    ds = (probs[j] * (dps[j] - delta)).astype(BF16)
                    sum_q += nn(ds, k_ref[there, kv])
                    dk[there, kv] += tn(ds, query)
                    dv[there, kv] += tn(probs[j].astype(BF16), grad)
                dq[here, cols] = sum_q
        for p in range(count):
            at = pl.ds(pl.multiple_of(base[p], piece), piece)
            to = slice(p * piece, (p + 1) * piece)
            cos, sin = cos_ref[at, :], sin_ref[at, :]
            for src, wide, start in ((dq, width, 0), (dk, kv_width, width)):
                for h in range(wide // HD):
                    w = src[at, h * HD : (h + 1) * HD] * factor
                    turned = w * cos - pltpu.roll(w, HD // 2, 1) * sin
                    out[to, start + h * HD : start + (h + 1) * HD] = turned.astype(BF16)
            out[to, width + kv_width :] = dv[at, :].astype(BF16)

    return order.call(
        body,
        (*qs, *lses, grads, k_all, v_all, *tables),
        [spec((total, width + 2 * kv_width))],
        smem=(bases,),
        scratch=[
            pltpu.VMEM((total, width), BF16),
            pltpu.VMEM((total, heads), F32),
            pltpu.VMEM((total, width), F32),
            pltpu.VMEM((total, kv_width), F32),
            pltpu.VMEM((total, kv_width), F32),
        ],
    )[0]


def back_one(order, grads, weights, bases, piece, step=512):
    rows, total = grads.shape
    depth = weights[0].shape[0]
    edges = [0]
    for w in weights:
        edges.append(edges[-1] + w.shape[1])

    def body(base, g_ref, *refs):
        value = sum(
            nt(g_ref[:, edges[i] : edges[i + 1]], refs[i][...]) for i in range(len(weights))
        )
        put_pieces(refs[-1], value, base, piece)

    return order.call(
        body,
        (grads, *weights),
        [spec((rows, depth))],
        smem=(bases,),
        grid=(depth // step,),
        ins=[VMEM] + [pl.BlockSpec((step, w.shape[1]), lambda i: (i, 0)) for w in weights],
        outspecs=[pl.BlockSpec((rows, step), lambda i: (0, i))],
    )[0]


class Job:
    def __init__(self, groups, outs, halves):
        self.groups, self.outs = groups, outs
        self.pairs = [pair for group in groups for pair in group]
        self.rows = self.pairs[0][0][0].shape[1]
        self.chunks, at = [], 0
        for half in halves:
            self.chunks.append((at, half))
            at += 2 * half
        self.widths = [sum(n for _, right, _ in group for _, _, n in right[:1]) for group in groups]
        self.results = [() for _ in groups]
        self.got = {}


def product(order, job, pick, chunks, bases, piece, add_to=None):
    start, half = job.chunks[chunks[0]]
    first, count, many = start // half, len(chunks), len(job.groups)
    width = job.widths[0]
    lefts, places = [], []
    for left, _, _ in job.pairs:
        if not any(left is known for known, _ in places):
            places.append((left, len(lefts)))
            lefts += left
    rights = [window for _, right, _ in job.pairs for window in right]
    total = sum(p.shape[0] for p in job.pairs[0][0])
    extra = 0 if add_to is None else 1
    got_array, got_at = add_to if extra else (None, 0)

    def body(pick_ref, base, *refs):
        left_refs, refs = refs[: len(lefts)], refs[len(lefts) :]
        right_refs, refs = refs[: len(rights)], refs[len(rights) :]
        got, outs, whole = refs[:extra], refs[extra:-1], refs[-1]

        @pl.when(pl.program_id(0) == 0)
        def _():
            at, n = 0, 0
            for _, right, placed in job.pairs:
                wide = right[0][2]
                value = stack(right_refs[n : n + len(right)])
                here = slice(at, at + wide)
                if placed:
                    put_pieces(whole, value, base, piece, here)
                else:
                    whole[:, here] = value
                at += wide
                n += len(right)

        stacks = {
            start: stack(left_refs[start : start + len(left)]) for left, start in places
        }
        at = 0
        for g, group in enumerate(job.groups):
            put = 0
            for left, right, _ in group:
                wide = right[0][2]
                start = next(s for known, s in places if known is left)
                value = tn(stacks[start], whole[:, at : at + wide])
                here = slice(put, put + wide)
                if extra:
                    mine = slice(g * half, (g + 1) * half)
                    value = (value + got[0][mine, here].astype(F32)).astype(BF16)
                    for i in range(count):

                        @pl.when(pl.program_id(0) == i)
                        def _():
                            outs[i * many + g][:, here] = value
                else:
                    outs[0][g * half : (g + 1) * half, here] = value.astype(BF16)
                at += wide
                put += wide

    block = pl.BlockSpec((many * half, width), lambda i, pick_ref, base: (i, 0))
    if extra:
        outs, outspecs = [spec((half, width))] * (count * many), None
    else:
        outs, outspecs = [spec((count * many * half, width))], [block]
    return order.call(
        body,
        (*lefts, *[array for array, _, _ in rights], *([got_array] if extra else [])),
        outs,
        prefetch=(pick, bases),
        grid=(count,),
        ins=[
            pl.BlockSpec((p.shape[0], half), lambda i, pick_ref, base: (0, first + 2 * i + pick_ref[0]))
            for p in lefts
        ]
        + [
            pl.BlockSpec((array.shape[0], n), lambda i, pick_ref, base, at=at // n: (0, at))
            for array, at, n in rights
        ]
        + [
            pl.BlockSpec((many * half, width), lambda i, pick_ref, base: (i + got_at, 0))
        ]
        * extra,
        outspecs=outspecs,
        scratch=[pltpu.VMEM((total, sum(job.widths)), BF16)],
    )


def lay(order, job, group, core, chunk, mine, other):
    start, half = job.chunks[chunk]

    def body(core_ref, mine_ref, other_ref, *outs):
        for n, ref in ((0, mine_ref), (1, other_ref)):

            @pl.when(pl.program_id(0) == n)
            def _():
                for (at, width, turned, _, _), out in zip(job.outs[group], outs):
                    value = ref[:, at : at + width].astype(F32)
                    out[...] = value.T if turned else value

    shapes, specs = [], []
    for _, width, turned, whole, place in job.outs[group]:
        if turned:
            shapes.append(pltpu.HBM((whole, job.rows), F32))
            specs.append(
                pl.BlockSpec(
                    (width, half),
                    lambda n, core_ref, p=place: (p, start // half + (core_ref[0] ^ n)),
                )
            )
        else:
            shapes.append(pltpu.HBM((job.rows, whole), F32))
            specs.append(
                pl.BlockSpec(
                    (half, width),
                    lambda n, core_ref, p=place: (start // half + (core_ref[0] ^ n), p),
                )
            )
    job.results[group] = order.call(
        body,
        (mine, other),
        shapes,
        prefetch=(core,),
        grid=(2,),
        outspecs=specs,
        reuse=job.results[group],
    )


class Line:
    LAG = 2

    def __init__(self, order, size, bases, piece):
        self.order, self.size, self.bases, self.piece = order, size, bases, piece
        where = lax.axis_index("dp")
        core, z = where % 2, where // 2
        self.mine = core.reshape(1).astype(jnp.int32)
        self.other = (1 - core).reshape(1).astype(jnp.int32)
        self.middle = ((z == 1) | (z == 2)).astype(jnp.int32).reshape(1)
        self.count = 0
        self.chunks = []
        self.part, self.fold, self.half, self.mids = [], {}, {}, {}
        self.whole, self.ends, self.final, self.done = {}, {}, {}, {}

    def hop(self, value, steps):
        pairs = [(2 * a + c, 2 * b + c) for a, b in steps for c in range(2)]
        return lax.ppermute(value, "dp", pairs)

    def send(self, job, chunks):
        part = product(self.order, job, self.other, chunks, self.bases, self.piece)[0]
        got = swap(part, "dp", self.size, 1)
        for n, k in enumerate(chunks):
            job.got[k] = (got, n)

    def enter(self, job, chunks):
        got = job.got[chunks[0]]
        parts = iter(product(self.order, job, self.mine, chunks, self.bases, self.piece, got))
        for k in chunks:
            for group in range(len(job.groups)):
                part = next(parts)
                n = len(self.part)
                if n < 2 * self.LAG:
                    self.fold[n] = self.hop(part, [(0, 1), (3, 2)])
                self.chunks.append((job, group, k))
                self.part.append(part)

    def tick(self, k):
        b, c, ahead = k - self.LAG, k - 2 * self.LAG, k + self.LAG
        here, back, out = k < self.count, 0 <= b < self.count, 0 <= c < self.count
        on = 2 * self.LAG <= ahead < self.count
        merged = back and on and self.half[b].shape == self.part[ahead].shape
        operands, outs = [], []
        if here:
            operands += [self.part[k], self.fold[k]]
            outs.append(spec(self.part[k].shape))
        if back:
            operands += [self.half[b], self.mids[b]]
            outs.append(spec(self.half[b].shape))
        if merged:
            operands.append(self.part[ahead])
        if out:
            operands += [self.whole[c], self.ends[c]]
            outs.append(spec(self.whole[c].shape))

        def body(flag, *refs):
            middle = flag[0] != 0
            refs, results = list(refs[: len(operands)]), list(refs[len(operands) :])
            if here:
                results.pop(0)[...] = plus(refs.pop(0), refs.pop(0)).astype(BF16)
            if back:
                both = plus(refs.pop(0), refs.pop(0)).astype(BF16)
                results.pop(0)[...] = jnp.where(middle, both, refs.pop(0)[...]) if merged else both
            if out:
                results.pop(0)[...] = jnp.where(middle, refs.pop(0)[...], refs.pop(0)[...])

        wait = [self.done[c - 1]] if c - 1 in self.done else []
        got = list(pointwise(self.order, body, operands, outs, smem=(self.middle,), wait=wait))
        if here:
            self.half[k] = got.pop(0)
        if back:
            self.whole[b] = got.pop(0)
        if out:
            self.final[c] = got.pop(0)
        if here:
            self.mids[k] = self.hop(self.half[k], [(1, 2), (2, 1)])
        if merged:
            both = self.hop(self.whole[b], [(0, 1), (1, 0), (2, 3), (3, 2)])
            self.ends[b] = self.fold[ahead] = both
        else:
            if back:
                self.ends[b] = self.hop(self.whole[b], [(1, 0), (2, 3)])
            if on:
                part = self.order.tie(self.part[ahead])
                self.fold[ahead] = self.hop(part, [(0, 1), (3, 2)])
        if out:
            self.done[c] = swap(self.final[c], "dp", self.size, 1)

    def lay(self, i):
        if 0 <= i < self.count:
            job, group, k = self.chunks[i]
            lay(self.order, job, group, self.mine, k, self.final[i], self.done[i])


class SmallSum:
    def __init__(self, order, value, mesh_shape):
        self.order, self.value = order, value
        self.steps = []
        for axis in ("tensor", "dp"):
            size, bit = mesh_shape[axis], 1
            if size & (size - 1):
                self.steps.append((axis, size, None))
                continue
            while bit < size:
                self.steps.append((axis, size, bit))
                bit *= 2

    def step(self):
        if self.steps:
            axis, size, bit = self.steps.pop(0)
            if bit is None:
                self.value = lax.psum(self.value, axis)
            else:
                self.value = add(self.order, self.value, swap(self.value, axis, size, bit))


def local(
    mesh_shape,
    tokens,
    cotangent,
    w_query,
    w_key,
    w_value,
    w_output,
    w_gate,
    w_up,
    w_down,
    gain_attn,
    gain_mlp,
    dropped,
    exit_scale,
    positions,
):
    x, ct = tokens[0], cotangent[0]
    order = Order()
    square = mesh_shape["tensor"] == 4 and mesh_shape["dp"] == 8
    rows = Rows(mesh_shape["tensor"], x.shape[0], square)
    bases = rows.bases
    line = Line(order, mesh_shape["dp"], bases, rows.piece)
    pieces = 2 if square else 1
    scal = jnp.stack([1.0 - dropped[0].astype(F32), exit_scale[0]])
    gain_one, gain_two = gain_attn[None], gain_mlp[None]
    attn_weights = (w_query, w_key, w_value)

    freqs = jnp.exp(jnp.arange(HD // 2, dtype=F32) * (-2.0 * math.log(10000.0) / HD))
    turned = positions[0].astype(F32)[:, None] * freqs[None, :]
    cos, sin = jnp.cos(turned), jnp.sin(turned)
    tables = (jnp.concatenate([cos, cos], axis=1), jnp.concatenate([-sin, sin], axis=1))

    n_own, grad_m_own = prepare(order, x, ct, gain_one, scal, pieces)
    qs, ks, vs = {}, {}, {}

    def project_group(group, n_one):
        last = group is rows.groups[-1]
        done = [(ks[i], vs[i]) for i in sorted(ks)] if last else None
        got = project(
            order, [n_one[i] for i in group], attn_weights, tables, bases, group, done
        )
        for n, i in enumerate(group):
            qs[i], ks[i], vs[i] = got[n], got[2 + n], got[4 + n]
        return got[6:]

    if square:
        n_one = rows.gather_first(n_own)
        project_group(rows.groups[0], n_one)
        n_one += rows.gather_second(order.tie(*n_own))
        n_one += rows.gather_third(*order.tie(n_one[2], n_one[3]))
        project_group(rows.groups[1], n_one)
        project_group(rows.groups[2], n_one)
        grad_m = rows.gather_all(order.tie(grad_m_own))
        k_all, v_all = project_group(rows.groups[3], n_one)
    else:
        n_one = rows.gather_whole(n_own[0])
        grad_m = rows.gather_all(grad_m_own)
        for group in rows.groups:
            k_all, v_all = project_group(group, n_one) or (None, None)

    attn, lses, parts = {}, {}, {}

    def attend_block(block):
        got = attend(order, [qs[i] for i in block], k_all, v_all, w_output, bases, block[0])
        for n, i in enumerate(block):
            attn[i], lses[i], parts[i] = got[n], got[2 + n], got[4 + n]

    out_sum = Scatter(order, rows)
    if square:
        attend_block(rows.blocks[0])
        out_sum.far({i: parts[i] for i in (6, 7)})
        attend_block(rows.blocks[1])
        attend_block(rows.blocks[2])
        out_sum.near({i: parts[i] for i in (2, 3)})
        out_sum.rest({i: parts[i] for i in (4, 5)})
        attend_block(rows.blocks[3])
        out_sum.own({i: parts[i] for i in (0, 1)})
    else:
        for block in rows.blocks:
            attend_block(block)
        out_sum.own(parts)
    h_one, n_two_own = second_norm(order, x, out_sum.result(), gain_two, scal, pieces)

    hidden, dgate, dup = [], [], []
    dhid = back_hidden(order, grad_m, w_down)

    def feed(g):
        group = rows.groups[g]
        got = feed_forward(
            order, [n_two[i] for i in group], dhid, w_gate, w_up, bases, group
        )
        for made, values in zip(got, (hidden, dgate, dup)):
            values.append(made)

    every = range(rows.count)
    if square:
        n_two = rows.gather_first(n_two_own)
        n_two += rows.gather_second(n_two_own)
        feed(0)
        n_two += rows.gather_third(*order.tie(n_two[2], n_two[3]))
        feed(1)
        feed(2)
        feed(3)
    else:
        n_two = rows.gather_whole(n_two_own[0])
        for g in range(len(rows.groups)):
            feed(g)

    def back_two_all():
        return rows.scatter_all(
            back_two(order, dgate, dup, w_gate, w_up, bases, rows.piece)
        )

    def second_back_all(total):
        return second_back(order, h_one, ct, total, gain_two, scal)

    def attend_back_all(grad_a):
        return attend_back(
            order,
            [qs[i] for i in every],
            k_all,
            v_all,
            back_out(order, grad_a, w_output),
            [lses[i] for i in every],
            tables,
            bases,
        )

    def back_one_all(gqkv):
        return rows.scatter_all(back_one(order, gqkv, attn_weights, bases, rows.piece))

    def down_all():
        return rows.scatter_all(down_rows(order, hidden, w_down, bases, rows.piece))

    ff, width, kv = w_gate.shape[1], w_query.shape[1], w_key.shape[1]
    def whole_of(arrays):
        return [(array, 0, array.shape[1]) for array in arrays]

    ff_out = [[(0, ff, False, ff, 0)]]
    down = Job([[([grad_m], whole_of(hidden), True)]], [[(0, ff, True, ff, 0)]], [256] * 4)
    wide = Job(
        [[(n_two, whole_of(dgate), False)], [(n_two, whole_of(dup), False)]],
        ff_out * 2,
        [256] * 4,
    )

    def late_jobs(grad_a, gqkv):
        total = gqkv.shape[1]
        rest = HD if square else 0
        right = [(gqkv, 0, total - rest)]
        outs = [
            (0, width, True, width, 0),
            (width, width, False, width, 0),
            (2 * width, kv, False, kv, 0),
            (2 * width + kv, kv - rest, False, kv, 0),
        ]
        pairs = [([grad_a], whole_of([attn[i] for i in every]), True), (n_one, right, False)]
        jobs = [Job([pairs], [outs], [256, 256, 256, 128, 128])]
        if rest:
            pairs = [(n_one, [(gqkv, total - rest, rest)], False)]
            jobs.append(Job([pairs], [[(0, rest, False, kv, kv // rest - 1)]], [1024]))
        return jobs

    if square:
        line.count = 18
        line.send(down, [0, 1])
        line.send(down, [2, 3])
        line.enter(down, [0])
        two_total = back_two_all()
        line.enter(down, [1])
        line.send(wide, [0, 1])
        line.tick(0)
        line.enter(down, [2, 3])
        line.tick(1)
        line.enter(wide, [0, 1])
        line.tick(2)
        line.send(wide, [2, 3])
        line.tick(3)
        dh, gain_two_sum, grad_a_own = second_back_all(two_total)
        grad_a = rows.gather_all(grad_a_own)
        line.tick(4)
        line.enter(wide, [2, 3])
        line.tick(5)
        mix_total = down_all()
        line.tick(6)
        line.lay(0)
        line.tick(7)
        gqkv = attend_back_all(grad_a)
        late, late_rest = late_jobs(grad_a, gqkv)
        line.tick(8)
        line.send(late, [0, 1, 2])
        one_total = back_one_all(gqkv)
        line.tick(9)
        line.enter(late, [0, 1, 2])
        line.tick(10)
        line.send(late, [3, 4])
        line.send(late_rest, [0])
        line.tick(11)
        line.lay(1)
        line.enter(late, [3, 4])
        line.enter(late_rest, [0])
        line.tick(12)
        line.lay(2)
        line.lay(3)
        line.tick(13)
        line.lay(4)
        line.lay(5)
        laid = 6
        for k in range(14, line.count + 2 * line.LAG):
            line.tick(k)
            if k == 14:
                mixed = mix(order, h_one, mix_total, scal)
                input_grad, gain_one_sum = first_back(order, x, dh, one_total, gain_one)
                gains = SmallSum(
                    order, jnp.concatenate([gain_one_sum, gain_two_sum]), mesh_shape
                )
            while laid <= min(k - 5, laid + 2) and laid < 6 + 2 * (k - 13):
                line.lay(laid)
                laid += 1
            if k in (15, 16, 17, 18, 20):
                gains.step()
        while laid < line.count - 1:
            line.lay(laid)
            laid += 1
        late_rest.results[0] = (late.results[0][3],)
        line.lay(line.count - 1)
        gain_sums = gains.value
    else:
        dh, gain_two_sum, grad_a_own = second_back_all(back_two_all())
        grad_a = rows.gather_all(grad_a_own)
        gqkv = attend_back_all(grad_a)
        (late,) = late_jobs(grad_a, gqkv)
        mixed = mix(order, h_one, down_all(), scal)
        input_grad, gain_one_sum = first_back(order, x, dh, back_one_all(gqkv), gain_one)
        gains = SmallSum(order, jnp.concatenate([gain_one_sum, gain_two_sum]), mesh_shape)
        while gains.steps:
            gains.step()
        gain_sums = gains.value
        for job in (down, wide, late):
            for n, group in enumerate(job.groups):
                parts = [
                    tn(jnp.concatenate(a), jnp.concatenate([array for array, _, _ in b]))
                    for a, b, _ in group
                ]
                whole = jnp.concatenate(parts, axis=1).astype(BF16)
                whole = lax.psum(whole, "dp").astype(F32)
                job.results[n] = [
                    whole[:, at : at + size].T if turned else whole[:, at : at + size]
                    for at, size, turned, _, _ in job.outs[n]
                ]
    grad_output, grad_query, grad_key, grad_value = late.results[0]
    if square:
        grad_value = late_rest.results[0][0]
    return (
        mixed[None],
        input_grad[None],
        grad_query,
        grad_key,
        grad_value,
        grad_output,
        wide.results[0][0],
        wide.results[1][0],
        down.results[0][0],
        gain_sums[0],
        gain_sums[1],
    )


def solution(mesh):
    shape = dict(mesh.shape)
    placed = (
        P("dp", "tensor", None),
        P("dp", "tensor", None),
        P(None, "tensor"),
        P(None, "tensor"),
        P(None, "tensor"),
        P("tensor", None),
        P(None, "tensor"),
        P(None, "tensor"),
        P("tensor", None),
        P(),
        P(),
        P("dp"),
        P("dp"),
        P("dp", None),
    )

    def step(*args):
        return local(shape, *args)

    return jax.shard_map(
        step,
        mesh=mesh,
        in_specs=placed,
        out_specs=(
            P("dp", "tensor", None),
            P("dp", "tensor", None),
            P(None, "tensor"),
            P(None, "tensor"),
            P(None, "tensor"),
            P("tensor", None),
            P(None, "tensor"),
            P(None, "tensor"),
            P("tensor", None),
            P(),
            P(),
        ),
        check_vma=False,
    )
```
